256 devices in a mesh: head: 4 (over x), inner: 8 (over z_lo, y), outer: 8 (over z_hi, core).
Axes of the slice: x: 4, y: 4, z: 8 (z_hi: 4, z_lo: 2; z = z_hi * 2 + z_lo), core: 2. Of those that a mesh axis runs over, the one named last changes fastest.
Arguments:
- query_heads: bfloat16 [16384, 3072], P(('inner', 'outer', 'head')), may hold values from -256 to 256
- key_heads: bfloat16 [16384, 512], P(('inner', 'outer', 'head')), may hold values from -6 to 6
- value_matrix: bfloat16 [16384, 512], P(('inner', 'outer', 'head')), may hold values from -6 to 6
- out_grad: bfloat16 [16384, 3072], P(('inner', 'outer', 'head')), may hold values from -6 to 6
- segment_ids: int32 [16384], replicated, may hold values from 0 to 63, never falling along the last dimension, each value on 1 to 1792 neighbouring positions
Outputs:
- query_grad: bfloat16 [16384, 3072], P(('inner', 'outer', 'head'))
- key_grad: bfloat16 [16384, 512], P(('inner', 'outer', 'head'))
- value_grad: bfloat16 [16384, 512], P(('inner', 'outer', 'head'))
The draws below stay inside these ranges and needn't reach their ends.
Inputs may be any that keep to these rules, and one draw needn't show every extreme that they name: `segment_ids`: session ids never fall along the sequence; each session covers at most 1792 positions, and one covers exactly that many.
All inputs are finite; a program needn't handle non-finite values.
Results may differ from the reference program's by a relative error of at most 0.019.
Values may be sent and summed in bfloat16 or wider, within the bound.
A program may use at most 64 MiB of HBM per device.

```python
import math
import jax
import jax.numpy as jnp
import numpy as np
from jax import lax

HEAD_SIZE = 128
QUERY_HEADS = 24
KEY_VALUE_HEADS = 4
PACKED_TOKENS = 16384
LONGEST = 1792


def shared_keys(key):
    return jnp.clip(jax.random.normal(key, (PACKED_TOKENS, KEY_VALUE_HEADS * HEAD_SIZE), jnp.float32), -6.0, 6.0)


def draw_key_heads(key, part):
    base_offset = shared_keys(key)
    return base_offset.astype(jnp.bfloat16)


def draw_query_heads(key, part):
    key = jax.random.fold_in(key, 5)
    fresh = jnp.clip(jax.random.normal(key, (PACKED_TOKENS, QUERY_HEADS * HEAD_SIZE), jnp.float32), -6.0, 6.0)
    return fresh.astype(jnp.bfloat16)


def shard_levels(key, shape, cuts, low, top_value):
    level, own = 1.0, jax.random.fold_in(key, 6)
    for dim, shards_of in cuts:
        draws = jnp.exp(jax.random.uniform(jax.random.fold_in(own, dim), (shards_of,), jnp.float32, low / len(cuts), top_value / len(cuts)))
        level = level * jnp.repeat(draws, shape[dim] // shards_of).reshape([-1 if axis == dim else 1 for axis in range(len(shape))])
    return level


def length_profile(amount, total, reach, slope):
    weights = [(1 << 20) // math.isqrt(grade ** slope) + 1 for grade in range(2, amount + 1)]
    rest, counts = total - reach - (amount - 1), [1] * (amount - 1)
    while rest > 0:
        free = [i for i in range(amount - 1) if counts[i] < reach]
        pool, remaining = sum([weights[i] for i in free]), rest
        for i in free:
            more = min(reach - counts[i], max(1, remaining * weights[i] // pool), rest)
            counts[i] = counts[i] + more
            rest = rest - more
    return np.array([reach] + counts)


def uneven(stream_key, count, total, bound, lean):
    if count == 2:
        one = jax.random.randint(stream_key, (), max(1, total - bound), min(bound, total - 1) + 1)
        return jnp.stack([one, total - one])
    lengths = jnp.asarray(length_profile(count, total, bound, lean), jnp.int32)
    twos = (count - 1) // 2
    source_of, taker = lengths[1:1 + 2 * twos:2], lengths[2:2 + 2 * twos:2]
    room = jnp.minimum(source_of - 1, bound - taker)
    shifted = jax.random.randint(jax.random.fold_in(stream_key, 1), (twos,), 0, 1 << 20) % (room + 1)
    lengths = lengths.at[1:1 + 2 * twos:2].set(source_of - shifted).at[2:2 + 2 * twos:2].set(taker + shifted)
    return lengths[jax.random.permutation(jax.random.fold_in(stream_key, 2), count)]


def noise(stream_key, shape, spread, bound, shards=(), kind=jnp.bfloat16):
    factor_of = shard_levels(stream_key, shape, shards, -0.22, 0.18) if shards else 1.0
    result = jax.random.normal(stream_key, shape, jnp.float32) * spread * factor_of
    return jnp.minimum(jnp.maximum(result, -bound), bound).astype(kind)


def setup_inputs(seed: int = 0) -> dict:
    arg_keys = jax.random.split(jax.random.key(seed), 6)
    query_heads = draw_query_heads(jax.random.fold_in(arg_keys[5], 71), 0)
    key_heads = draw_key_heads(jax.random.fold_in(arg_keys[5], 71), 0)
    value_matrix = noise(arg_keys[2], (PACKED_TOKENS, KEY_VALUE_HEADS * HEAD_SIZE), 1.0, 6.0, ((0, 256),))
    out_grad = noise(arg_keys[3], (PACKED_TOKENS, QUERY_HEADS * HEAD_SIZE), 1.0, 6.0, ((0, 256),))
    segment_ids = jnp.searchsorted(jnp.cumsum(uneven(arg_keys[4], max(16, PACKED_TOKENS // 256), PACKED_TOKENS, LONGEST, 2)), jnp.arange(PACKED_TOKENS), side="right").astype(jnp.int32)
    return dict(query_heads=query_heads, key_heads=key_heads, value_matrix=value_matrix, out_grad=out_grad, segment_ids=segment_ids)


NEG_FILL = -1e30


def head_grads(query_group, key_one, value_one, grad_group, segment_ids, score_scale):
    block = math.gcd(512, PACKED_TOKENS)
    group_index = QUERY_HEADS // KEY_VALUE_HEADS
    span_len = min(PACKED_TOKENS, LONGEST + block)
    key_wide = key_one.astype(jnp.float32)
    value_wide = value_one.astype(jnp.float32)

    def step(carry, block_start):
        key_acc, value_acc = carry
        key_start = jnp.clip(block_start - LONGEST, 0, PACKED_TOKENS - span_len).astype(jnp.int32)
        query_block = lax.dynamic_slice_in_dim(query_group, block_start, block, 0).astype(jnp.float32)
        grad_block = lax.dynamic_slice_in_dim(grad_group, block_start, block, 0).astype(jnp.float32)
        query_pos = block_start + jnp.arange(block, dtype=jnp.int32)
        query_seg = lax.dynamic_slice_in_dim(segment_ids, block_start, block, 0)
        key_pos = key_start + jnp.arange(span_len, dtype=jnp.int32)
        key_seg = lax.dynamic_slice_in_dim(segment_ids, key_start, span_len, 0)
        key_part = lax.dynamic_slice_in_dim(key_wide, key_start, span_len, 0)
        value_part = lax.dynamic_slice_in_dim(value_wide, key_start, span_len, 0)
        allowed = (key_pos[None, :] <= query_pos[:, None]) & (key_seg[None, :] == query_seg[:, None])
        allowed = allowed[:, None, :]
        scores = jnp.einsum("rgd,cd->rgc", query_block, key_part) * score_scale
        masked = jnp.where(allowed, scores, NEG_FILL)
        row_top = jnp.max(masked, axis=-1, keepdims=True)
        row_total = jnp.sum(jnp.where(allowed, jnp.exp(masked - row_top), 0.0), axis=-1, keepdims=True)
        lse = row_top + jnp.log(row_total)
        probs = jnp.where(allowed, jnp.exp(masked - lse), 0.0)
        prob_grads = jnp.einsum("rgd,cd->rgc", grad_block, value_part)
        delta = jnp.sum(probs * prob_grads, axis=-1, keepdims=True)
        score_grads = lax.optimization_barrier((probs * (prob_grads - delta)).astype(jnp.bfloat16)).astype(jnp.float32)
        probs_half = lax.optimization_barrier(probs.astype(jnp.bfloat16)).astype(jnp.float32)
        query_out = score_scale * jnp.einsum("rgc,cd->rgd", score_grads, key_part)
        key_add = score_scale * jnp.einsum("rgc,rgd->cd", score_grads, query_block)
        value_add = jnp.einsum("rgc,rgd->cd", probs_half, grad_block)
        key_acc = lax.dynamic_update_slice_in_dim(key_acc, lax.dynamic_slice_in_dim(key_acc, key_start, span_len, 0) + key_add, key_start, 0)
        value_acc = lax.dynamic_update_slice_in_dim(value_acc, lax.dynamic_slice_in_dim(value_acc, key_start, span_len, 0) + value_add, key_start, 0)
        return (key_acc, value_acc), query_out.astype(jnp.bfloat16)

    starts = jnp.arange(PACKED_TOKENS // block, dtype=jnp.int32) * block
    zeros = jnp.zeros((PACKED_TOKENS, HEAD_SIZE), jnp.float32)
    (key_acc, value_acc), query_out = lax.scan(step, (zeros, zeros), starts)
    query_out = query_out.reshape(PACKED_TOKENS, group_index * HEAD_SIZE)
    return query_out, key_acc.astype(jnp.bfloat16), value_acc.astype(jnp.bfloat16)


def reference(query_heads, key_heads, value_matrix, out_grad, segment_ids):
    group_index = QUERY_HEADS // KEY_VALUE_HEADS
    score_scale = HEAD_SIZE ** -0.5
    query_parts = []
    key_parts = []
    value_parts = []
    for key_value_head in range(KEY_VALUE_HEADS):
        low = key_value_head * group_index * HEAD_SIZE
        high = (key_value_head + 1) * group_index * HEAD_SIZE
        query_group = query_heads[:, low:high].reshape(PACKED_TOKENS, group_index, HEAD_SIZE)
        grad_group = out_grad[:, low:high].reshape(PACKED_TOKENS, group_index, HEAD_SIZE)
        key_one = key_heads[:, key_value_head * HEAD_SIZE:(key_value_head + 1) * HEAD_SIZE]
        value_one = value_matrix[:, key_value_head * HEAD_SIZE:(key_value_head + 1) * HEAD_SIZE]
        query_out, key_out, value_out = head_grads(query_group, key_one, value_one, grad_group, segment_ids, score_scale)
        query_parts.append(query_out)
        key_parts.append(key_out)
        value_parts.append(value_out)
    return (jnp.concatenate(query_parts, axis=1), jnp.concatenate(key_parts, axis=1), jnp.concatenate(value_parts, axis=1))
```

```python
import functools

import jax
import jax.numpy as jnp
from jax import lax
from jax.experimental import pallas as pl
from jax.experimental.pallas import tpu as pltpu
from jax.sharding import PartitionSpec as P

HEAD_SIZE = 128
QUERY_HEADS = 24
KEY_VALUE_HEADS = 4
KINDS = 128
FAR = 1e30
LOG2_E = 1.4426950408889634
MESH = pl.DeviceIdType.MESH
CORES = 2

OTHER_2, SAME_2, OTHER_1, OTHER_3, EXTRA, SAME_3, SAME_1, SELF = range(8)
SLOTS = 8
CHIPS_BACK = {OTHER_2: 2, SAME_2: 2, OTHER_1: 1, OTHER_3: 3, SAME_3: 3, SAME_1: 1}


def kernel(
    sizes,
    q_in, k_in, v_in, g_in, seg_in,
    dq_out, dk_out, dv_out,
    seg, queries, grads, keys, values, keys_t, kinds, unkind,
    scores, pgrads, stats, ds_half, p_half, dq_t, dq_half,
    part, part_other, chain, shares, last,
    seg_sem, q_sem, g_sem, kv_sem, qg_send, kv_send, fwd_send, fwd_other_send,
    part_send, other_sem, chain_sem, share_sem, dq_send, dq_sem, last_send, last_sem,
):
    head_count, inner_count, outer_count, group = sizes
    head = lax.axis_index("head")
    inner = lax.axis_index("inner")
    outer = lax.axis_index("outer")
    core = outer % CORES
    per_inner = outer_count // CORES
    chips = inner_count * per_inner
    chip = inner * per_inner + outer // CORES
    shards = chips * CORES
    place = chip * CORES + core
    tokens = q_in.shape[0]
    rows = head_count * tokens

    def at_chip(step, on_core):
        to = (chip + step + chips) % chips
        return (head, to // per_inner, (to % per_inner) * CORES + on_core)

    def at_head(step):
        to = (head + step) % head_count
        return to, (to, inner, outer)

    def wait_for(ref, sem):
        pltpu.make_async_copy(ref, ref, sem).wait()

    def send(src, dst, send_sem, recv_sem, to):
        pltpu.make_async_remote_copy(
            src_ref=src, dst_ref=dst, send_sem=send_sem, recv_sem=recv_sem,
            device_id=to, device_id_type=MESH,
        ).start()

    other = at_chip(0, 1 - core)
    next_1, next_3 = at_chip(1, core), at_chip(3, core)
    back_1, back_3 = at_chip(-1, core), at_chip(-3, core)
    extra_to = at_chip(4 * core, 1 - core)
    extra_from = at_chip(-4 * (1 - core), 1 - core)

    load_seg = pltpu.make_async_copy(seg_in, seg, seg_sem)
    load_seg.start()

    barrier = pltpu.get_barrier_semaphore()
    partners = [at_head(step)[1] for step in range(1, head_count)]
    partners += [other, next_1, next_3, back_1, back_3]
    far = at_chip(8 * core - 4, 1 - core)
    for partner in partners + [far]:
        pl.semaphore_signal(barrier, inc=1, device_id=partner, device_id_type=MESH)
    pl.semaphore_wait(barrier, len(partners) + 1)

    mine = pl.ds(pl.multiple_of(head * tokens, tokens), tokens)

    def head_columns(number):
        return pl.ds(pl.multiple_of(number * HEAD_SIZE, HEAD_SIZE), HEAD_SIZE)

    for kind, (src, dst) in enumerate(((k_in, keys), (v_in, values))):
        for step in range(1, head_count):
            to, device = at_head(step)
            send(
                src.at[:, head_columns(to)], dst.at[SELF, mine, :],
                kv_send.at[kind], kv_sem.at[SELF, kind], device,
            )
        pltpu.make_async_copy(
            src.at[:, head_columns(head)], dst.at[SELF, mine, :], kv_sem.at[SELF, kind]
        ).start()

    def send_head(number, carry):
        target = pl.ds(pl.multiple_of(number * rows + head * tokens, tokens), tokens)
        for kind, (src, dst, sem) in enumerate(
            ((q_in, queries, q_sem), (g_in, grads, g_sem))
        ):
            for step in range(1, head_count):
                to, device = at_head(step)
                send(
                    src.at[:, head_columns(to * group + number)], dst.at[target, :],
                    qg_send.at[kind], sem.at[number], device,
                )
            pltpu.make_async_copy(
                src.at[:, head_columns(head * group + number)], dst.at[target, :], sem.at[number]
            ).start()
        return carry

    lax.fori_loop(0, group, send_head, 0)

    load_seg.wait()
    lanes = seg.shape[1]
    seg_rows = rows // lanes
    session = lax.broadcasted_iota(jnp.int32, (KINDS, lanes), 0)

    def shard_of(slot):
        if slot == SELF:
            return place
        if slot == EXTRA:
            return (place - 7 + 6 * core + shards) % shards
        on_core = core if slot in (SAME_1, SAME_2, SAME_3) else 1 - core
        return ((chip - CHIPS_BACK[slot] + chips) % chips) * CORES + on_core

    for slot in range(SLOTS):
        for part_row in range(seg_rows):
            ids = seg[pl.ds(shard_of(slot) * seg_rows + part_row, 1), :]
            ones = jnp.where(session == ids, 1.0, 0.0).astype(jnp.float32).T
            span = slice(part_row * lanes, (part_row + 1) * lanes)
            kinds[slot, span, :] = ones.astype(jnp.bfloat16)
            if slot == SELF:
                unkind[span, :] = ((ones - 1.0) * FAR).astype(jnp.bfloat16)

    def turn_keys(slot):
        keys_t[slot] = keys[slot].astype(jnp.float32).T.astype(jnp.bfloat16)

    both = ((0, keys), (1, values))
    for kind, array in both:
        wait_for(array.at[SELF], kv_sem.at[SELF, kind])
        for number, (slot, to) in enumerate(((SAME_1, next_1), (SAME_3, next_3), (EXTRA, extra_to))):
            send(
                array.at[SELF], array.at[slot],
                fwd_send.at[number, kind], kv_sem.at[slot, kind], to,
            )

    turn_keys(SELF)

    def hand_over(slot, slot_there, number, kind, array):
        send(
            array.at[slot], array.at[slot_there],
            fwd_other_send.at[number, kind], kv_sem.at[slot_there, kind], other,
        )

    for kind, array in both:
        for slot, slot_there, number, owner, to in (
            (SAME_1, OTHER_1, 0, 0, next_1),
            (SAME_3, OTHER_3, 1, 1, back_1),
        ):
            wait_for(array.at[slot], kv_sem.at[slot, kind])
            if kind == owner:
                send(
                    array.at[slot], array.at[SAME_2],
                    fwd_send.at[3, kind], kv_sem.at[SAME_2, kind], to,
                )
            hand_over(slot, slot_there, number, kind, array)
    turn_keys(SAME_1)
    turn_keys(SAME_3)
    for kind, array in both:
        wait_for(array.at[SAME_2], kv_sem.at[SAME_2, kind])
        hand_over(SAME_2, OTHER_2, 2, kind, array)
    turn_keys(SAME_2)
    for slot in (EXTRA, OTHER_1, OTHER_3, OTHER_2):
        for kind, array in both:
            wait_for(array.at[slot], kv_sem.at[slot, kind])
        turn_keys(slot)

    score_scale = HEAD_SIZE ** (-0.5)
    over_last = (((1,), (1,)), ((), ()))

    def folded(block):
        return block.reshape(rows // 8, 8, rows)

    def head_span(number):
        return pl.ds(pl.multiple_of(number * rows, rows), rows)

    def forward(number, carry):
        wait_for(queries.at[head_span(number), :], q_sem.at[number])
        wait_for(grads.at[head_span(number), :], g_sem.at[number])

        def products(slot):
            wide_keys = jnp.concatenate([keys[slot], kinds[slot]], axis=1)
            wide_queries = jnp.concatenate([queries[head_span(number), :], unkind[...]], axis=1)
            block = lax.dot_general(
                wide_keys, wide_queries, over_last, preferred_element_type=jnp.float32
            )
            pgrads[slot, number] = lax.dot_general(
                values[slot], grads[head_span(number), :], over_last,
                preferred_element_type=jnp.float32,
            )
            return block

        def top_of(slot, top):
            block = products(slot)
            scores[slot, number] = block
            return jnp.maximum(top, jnp.max(folded(block), axis=0))

        block = products(SELF)
        key_row = lax.broadcasted_iota(jnp.int32, (rows, rows), 0)
        query_column = lax.broadcasted_iota(jnp.int32, (rows, rows), 1)
        block = jnp.where(key_row <= query_column, block, -FAR)
        scores[SELF, number] = block
        top = lax.fori_loop(0, SELF, top_of, jnp.max(folded(block), axis=0))
        top = jnp.max(top, axis=0, keepdims=True) * (score_scale * LOG2_E)

        def sums_of(slot, carry):
            total, cross = carry
            weights = jnp.exp2(scores[slot, number] * (score_scale * LOG2_E) - top)
            scores[slot, number] = weights
            total = total + jnp.sum(folded(weights), axis=0)
            cross = cross + jnp.sum(folded(weights * pgrads[slot, number]), axis=0)
            return total, cross

        zeros = jnp.zeros((8, rows), jnp.float32)
        total, cross = lax.fori_loop(0, SLOTS, sums_of, (zeros, zeros))
        inverse = 1.0 / jnp.sum(total, axis=0, keepdims=True)
        stats[number, 0:1, :] = inverse
        stats[number, 1:2, :] = jnp.sum(cross, axis=0, keepdims=True) * inverse
        return carry

    lax.fori_loop(0, group, forward, 0)

    dq_t[...] = jnp.zeros_like(dq_t)

    def backward(slot, carry):
        for number in range(group):
            probs = scores[slot, number] * stats[number, 0:1, :]
            span = slice(number * rows, (number + 1) * rows)
            p_half[:, span] = probs.astype(jnp.bfloat16)
            ds_half[:, span] = (probs * (pgrads[slot, number] - stats[number, 1:2, :])).astype(
                jnp.bfloat16
            )
        dk = jnp.dot(ds_half[...], queries[...], preferred_element_type=jnp.float32)
        dv = jnp.dot(p_half[...], grads[...], preferred_element_type=jnp.float32)
        dq_t[...] += jnp.dot(keys_t[slot], ds_half[...], preferred_element_type=jnp.float32)

        @pl.when((slot != SELF) & (slot != SAME_1) & (slot != SAME_2) & (slot != SAME_3))
        def _():
            part[slot, 0] = dk.astype(jnp.bfloat16)
            part[slot, 1] = dv.astype(jnp.bfloat16)

        for here, number in ((OTHER_2, 2), (OTHER_1, 0), (OTHER_3, 1)):

            @pl.when(slot == here)
            def _():
                send(
                    part.at[here], part_other.at[number], part_send.at[here],
                    other_sem.at[number], other,
                )

        @pl.when(slot == EXTRA)
        def _():
            send(
                part.at[EXTRA], shares.at[2], part_send.at[EXTRA], share_sem.at[2], extra_from
            )

        @pl.when(slot == SAME_2)
        def _():
            wait_for(part_other.at[2], other_sem.at[2])
            part[SAME_2, 0] = (dk + part_other[2, 0].astype(jnp.float32)).astype(jnp.bfloat16)
            part[SAME_2, 1] = (dv + part_other[2, 1].astype(jnp.float32)).astype(jnp.bfloat16)
            send(
                part.at[SAME_2, 0], chain.at[0], part_send.at[SAME_2], chain_sem.at[0], back_1
            )
            send(
                part.at[SAME_2, 1], chain.at[1], part_send.at[SAME_2], chain_sem.at[1], next_1
            )

        for here, number, kind, to in ((SAME_3, 1, 1, back_3), (SAME_1, 0, 0, back_1)):

            @pl.when(slot == here)
            def _():
                wait_for(part_other.at[number], other_sem.at[number])
                wait_for(chain.at[kind], chain_sem.at[kind])
                sums = [
                    dk + part_other[number, 0].astype(jnp.float32),
                    dv + part_other[number, 1].astype(jnp.float32),
                ]
                sums[kind] = sums[kind] + chain[kind].astype(jnp.float32)
                part[here, 0] = sums[0].astype(jnp.bfloat16)
                part[here, 1] = sums[1].astype(jnp.bfloat16)
                send(
                    part.at[here], shares.at[number], part_send.at[here],
                    share_sem.at[number], to,
                )

        @pl.when(slot == SELF)
        def _():
            last[0] = dk
            last[1] = dv

        return carry

    lax.fori_loop(0, SLOTS, backward, 0)

    def send_back(number, carry):
        dq = dq_t[:, head_span(number)].T * score_scale
        dq_half[head_span(number), :] = dq.astype(jnp.bfloat16)
        columns = head_columns(head * group + number)
        for step in range(1, head_count):
            to, device = at_head(step)
            here = pl.ds(pl.multiple_of(number * rows + to * tokens, tokens), tokens)
            send(dq_half.at[here, :], dq_out.at[:, columns], dq_send, dq_sem, device)
        here = pl.ds(pl.multiple_of(number * rows + head * tokens, tokens), tokens)
        pltpu.make_async_copy(dq_half.at[here, :], dq_out.at[:, columns], dq_sem).start()
        return carry

    lax.fori_loop(0, group, send_back, 0)

    for number in (2, 1, 0):
        wait_for(shares.at[number], share_sem.at[number])
    own = head_columns(head)
    for kind, out in enumerate((dk_out, dv_out)):
        total = last[kind]
        for number in range(3):
            total = total + shares[number, kind].astype(jnp.float32)
        if kind == 0:
            total = total * score_scale
        part[SELF, kind] = total.astype(jnp.bfloat16)
        for step in range(1, head_count):
            to, device = at_head(step)
            here = pl.ds(pl.multiple_of(to * tokens, tokens), tokens)
            send(
                part.at[SELF, kind, here, :], out.at[:, own],
                last_send.at[kind], last_sem.at[kind], device,
            )
        pltpu.make_async_copy(
            part.at[SELF, kind, mine, :], out.at[:, own], last_sem.at[kind]
        ).start()

    peers = head_count - 1
    for kind, (src, kv) in enumerate(((q_in, k_in), (g_in, v_in))):
        wait_for(src.at[:, : peers * group * HEAD_SIZE], qg_send.at[kind])
        wait_for(kv.at[:, : peers * HEAD_SIZE], kv_send.at[kind])
        array = (keys, values)[kind]
        for number in range(4):
            wait_for(array.at[SELF], fwd_send.at[number, kind])
        for number in range(3):
            wait_for(array.at[SELF], fwd_other_send.at[number, kind])
        wait_for(part.at[SELF, kind, : peers * tokens, :], last_send.at[kind])
    for slot in range(SELF):
        wait_for(part.at[slot], part_send.at[slot])
    wait_for(dq_out.at[:, : peers * group * HEAD_SIZE], dq_send)
    wait_for(dq_out, dq_sem)
    wait_for(dk_out, last_sem.at[0])
    wait_for(dv_out, last_sem.at[1])


def body(query_heads, key_heads, value_matrix, out_grad, segment_ids):
    head_count = lax.axis_size("head")
    sizes = (head_count, lax.axis_size("inner"), lax.axis_size("outer"), query_heads.shape[1] // key_heads.shape[1])
    group = sizes[3]
    tokens = query_heads.shape[0]
    rows = head_count * tokens
    half, full = jnp.bfloat16, jnp.float32
    ids = segment_ids.reshape(-1, 128)
    dma = pltpu.SemaphoreType.DMA
    anywhere = pl.BlockSpec(memory_space=pl.ANY)
    return pl.pallas_call(
        functools.partial(kernel, sizes),
        out_shape=(
            jax.ShapeDtypeStruct(query_heads.shape, half),
            jax.ShapeDtypeStruct(key_heads.shape, half),
            jax.ShapeDtypeStruct(value_matrix.shape, half),
        ),
        in_specs=[anywhere] * 5,
        out_specs=[anywhere] * 3,
        scratch_shapes=[
            pltpu.VMEM(ids.shape, jnp.int32),
            pltpu.VMEM((group * rows, HEAD_SIZE), half),
            pltpu.VMEM((group * rows, HEAD_SIZE), half),
            pltpu.VMEM((SLOTS, rows, HEAD_SIZE), half),
            pltpu.VMEM((SLOTS, rows, HEAD_SIZE), half),
            pltpu.VMEM((SLOTS, HEAD_SIZE, rows), half),
            pltpu.VMEM((SLOTS, rows, KINDS), half),
            pltpu.VMEM((rows, KINDS), half),
            pltpu.VMEM((SLOTS, group, rows, rows), full),
            pltpu.VMEM((SLOTS, group, rows, rows), full),
            pltpu.VMEM((group, 8, rows), full),
            pltpu.VMEM((rows, group * rows), half),
            pltpu.VMEM((rows, group * rows), half),
            pltpu.VMEM((HEAD_SIZE, group * rows), full),
            pltpu.VMEM((group * rows, HEAD_SIZE), half),
            pltpu.VMEM((SLOTS, 2, rows, HEAD_SIZE), half),
            pltpu.VMEM((3, 2, rows, HEAD_SIZE), half),
            pltpu.VMEM((2, rows, HEAD_SIZE), half),
            pltpu.VMEM((3, 2, rows, HEAD_SIZE), half),
            pltpu.VMEM((2, rows, HEAD_SIZE), full),
            dma,
            dma((group,)),
            dma((group,)),
            dma((SLOTS, 2)),
            dma((2,)),
            dma((2,)),
            dma((4, 2)),
            dma((3, 2)),
            dma((SLOTS,)),
            dma((3,)),
            dma((2,)),
            dma((3,)),
            dma,
            dma,
            dma((2,)),
            dma((2,)),
        ],
        compiler_params=pltpu.CompilerParams(
            collective_id=0, has_side_effects=True, vmem_limit_bytes=56 * 2**20
        ),
    )(query_heads, key_heads, value_matrix, out_grad, ids)


def solution(mesh):
    split = P(("inner", "outer", "head"), None)
    return jax.shard_map(
        body,
        mesh=mesh,
        in_specs=(split, split, split, split, P()),
        out_specs=(split, split, split),
        check_vma=False,
    )
```

```python
import functools

import jax
import jax.numpy as jnp
from jax import lax
from jax.experimental import pallas as pl
from jax.experimental.pallas import tpu as pltpu
from jax.sharding import PartitionSpec as P

HEAD_SIZE = 128
QUERY_HEADS = 24
KEY_VALUE_HEADS = 4
KINDS = 128
FAR = 1e30
LOG2_E = 1.4426950408889634
MESH = pl.DeviceIdType.MESH
CORES = 2

SELF, SAME_1, SAME_3, EXTRA, SAME_2, OTHER_1, OTHER_3, OTHER_2 = range(8)
SLOTS = 8
CHIPS_BACK = {OTHER_2: 2, SAME_2: 2, OTHER_1: 1, OTHER_3: 3, SAME_3: 3, SAME_1: 1}
SHARES = 4
KEY, VALUE = range(2)


def kernel(
    sizes,
    q_in, k_in, v_in, g_in, seg_in,
    dq_out, shares,
    seg, queries, grads, keys, values, keys_t, kinds, unkind,
    scores, pgrads, tops, sums, crosses, ds_half, p_half, dq_t, dq_half,
    fresh, hold, part, part_other, chain,
    seg_sem, q_sem, g_sem, kv_sem, qg_send, kv_send, fwd_send, fwd_other_send,
    part_send, other_sem, chain_sem, share_sem, dq_send, dq_sem,
):
    head_count, inner_count, outer_count, group = sizes
    head = lax.axis_index("head")
    inner = lax.axis_index("inner")
    outer = lax.axis_index("outer")
    core = outer % CORES
    per_inner = outer_count // CORES
    chips = inner_count * per_inner
    chip = inner * per_inner + outer // CORES
    shards = chips * CORES
    place = chip * CORES + core
    tokens = q_in.shape[0]
    rows = head_count * tokens

    def at_chip(step, on_core):
        to = (chip + step + chips) % chips
        return (head, to // per_inner, (to % per_inner) * CORES + on_core)

    def at_head(step):
        to = (head + step) % head_count
        return to, (to, inner, outer)

    def wait_for(ref, sem):
        pltpu.make_async_copy(ref, ref, sem).wait()

    def send(src, dst, send_sem, recv_sem, to):
        pltpu.make_async_remote_copy(
            src_ref=src, dst_ref=dst, send_sem=send_sem, recv_sem=recv_sem,
            device_id=to, device_id_type=MESH,
        ).start()

    other = at_chip(0, 1 - core)
    next_1, next_3 = at_chip(1, core), at_chip(3, core)
    back_1, back_3 = at_chip(-1, core), at_chip(-3, core)
    extra_to = at_chip(4 * core, 1 - core)
    extra_from = at_chip(-4 * (1 - core), 1 - core)

    load_seg = pltpu.make_async_copy(seg_in, seg, seg_sem)
    load_seg.start()

    barrier = pltpu.get_barrier_semaphore()
    partners = [at_head(step)[1] for step in range(1, head_count)]
    partners += [other, next_1, next_3, back_1, back_3]
    far = at_chip(8 * core - 4, 1 - core)
    for partner in partners + [far]:
        pl.semaphore_signal(barrier, inc=1, device_id=partner, device_id_type=MESH)
    pl.semaphore_wait(barrier, len(partners) + 1)

    mine = pl.ds(pl.multiple_of(head * tokens, tokens), tokens)

    def head_columns(number):
        return pl.ds(pl.multiple_of(number * HEAD_SIZE, HEAD_SIZE), HEAD_SIZE)

    for kind, (src, dst) in enumerate(((k_in, keys), (v_in, values))):
        for step in range(1, head_count):
            to, device = at_head(step)
            send(
                src.at[:, head_columns(to)], dst.at[SELF, mine, :],
                kv_send.at[kind], kv_sem.at[SELF, kind], device,
            )
        pltpu.make_async_copy(
            src.at[:, head_columns(head)], dst.at[SELF, mine, :], kv_sem.at[SELF, kind]
        ).start()

    def send_head(number, carry):
        target = pl.ds(pl.multiple_of(number * rows + head * tokens, tokens), tokens)
        for kind, (src, dst, sem) in enumerate(
            ((q_in, queries, q_sem), (g_in, grads, g_sem))
        ):
            for step in range(1, head_count):
                to, device = at_head(step)
                send(
                    src.at[:, head_columns(to * group + number)], dst.at[target, :],
                    qg_send.at[kind], sem.at[number], device,
                )
            pltpu.make_async_copy(
                src.at[:, head_columns(head * group + number)], dst.at[target, :], sem.at[number]
            ).start()
        return carry

    lax.fori_loop(0, group, send_head, 0)

    load_seg.wait()
    lanes = seg.shape[1]
    seg_rows = rows // lanes
    session = lax.broadcasted_iota(jnp.int32, (KINDS, lanes), 0)

    def shard_of(slot):
        if slot == SELF:
            return place
        if slot == EXTRA:
            return (place - 7 + 6 * core + shards) % shards
        on_core = core if slot in (SAME_1, SAME_2, SAME_3) else 1 - core
        return ((chip - CHIPS_BACK[slot] + chips) % chips) * CORES + on_core

    for slot in range(SLOTS):
        for part_row in range(seg_rows):
            ids = seg[pl.ds(shard_of(slot) * seg_rows + part_row, 1), :]
            ones = jnp.where(session == ids, 1.0, 0.0).astype(jnp.float32).T
            span = slice(part_row * lanes, (part_row + 1) * lanes)
            kinds[slot, span, :] = ones.astype(jnp.bfloat16)
            if slot == SELF:
                unkind[span, :] = ((ones - 1.0) * FAR).astype(jnp.bfloat16)

    both = ((KEY, keys), (VALUE, values))
    onward = {SAME_1: (0, next_1), SAME_3: (1, next_3), EXTRA: (2, extra_to)}

    def pass_on(slot, kind):
        number, to = onward[slot]
        array = both[kind][1]
        send(
            array.at[SELF], array.at[slot],
            fwd_send.at[number, kind], kv_sem.at[slot, kind], to,
        )

    def arrived(slot, kind):
        wait_for(both[kind][1].at[slot], kv_sem.at[slot, kind])

    arrived(SELF, KEY)
    pass_on(SAME_1, KEY)
    arrived(SELF, VALUE)
    pass_on(SAME_3, VALUE)
    pass_on(SAME_1, VALUE)
    pass_on(SAME_3, KEY)
    pass_on(EXTRA, KEY)
    pass_on(EXTRA, VALUE)

    def hand_over(slot, slot_there, number, kind):
        array = both[kind][1]
        send(
            array.at[slot], array.at[slot_there],
            fwd_other_send.at[number, kind], kv_sem.at[slot_there, kind], other,
        )

    def relay(slot, kind, to):
        array = both[kind][1]
        send(
            array.at[slot], array.at[SAME_2], fwd_send.at[3, kind], kv_sem.at[SAME_2, kind], to
        )

    arrived(SAME_1, KEY)
    relay(SAME_1, KEY, next_1)
    hand_over(SAME_1, OTHER_1, 0, KEY)
    arrived(SAME_3, VALUE)
    relay(SAME_3, VALUE, back_1)
    hand_over(SAME_3, OTHER_3, 1, VALUE)
    arrived(SAME_1, VALUE)
    hand_over(SAME_1, OTHER_1, 0, VALUE)
    arrived(SAME_3, KEY)
    hand_over(SAME_3, OTHER_3, 1, KEY)

    score_scale = HEAD_SIZE ** (-0.5)
    exponent = score_scale * LOG2_E
    over_last = (((1,), (1,)), ((), ()))

    def folded(block):
        return block.reshape(rows // 8, 8, rows)

    def head_span(number):
        return pl.ds(pl.multiple_of(number * rows, rows), rows)

    def forward(slot, masked):
        keys_t[slot] = keys[slot].astype(jnp.float32).T.astype(jnp.bfloat16)
        wide_keys = jnp.concatenate([keys[slot], kinds[slot]], axis=1)
        for number in range(group):
            span = slice(number * rows, (number + 1) * rows)
            wide_queries = jnp.concatenate([queries[span, :], unkind[...]], axis=1)
            block = lax.dot_general(
                wide_keys, wide_queries, over_last, preferred_element_type=jnp.float32
            )
            if masked:
                key_row = lax.broadcasted_iota(jnp.int32, (rows, rows), 0)
                query_column = lax.broadcasted_iota(jnp.int32, (rows, rows), 1)
                block = jnp.where(key_row <= query_column, block, -FAR)
            slopes = lax.dot_general(
                values[slot], grads[span, :], over_last, preferred_element_type=jnp.float32
            )
            top = jnp.max(jnp.max(folded(block), axis=0), axis=0, keepdims=True)
            weights = jnp.exp2((block - top) * exponent)
            scores[slot, number] = weights
            pgrads[slot, number] = slopes
            here = pl.ds(slot, 1)
            tops[number, here, :] = top
            sums[number, here, :] = jnp.sum(
                jnp.sum(folded(weights), axis=0), axis=0, keepdims=True
            )
            crosses[number, here, :] = jnp.sum(
                jnp.sum(folded(weights * slopes), axis=0), axis=0, keepdims=True
            )

    for number in range(group):
        wait_for(queries.at[head_span(number), :], q_sem.at[number])
        wait_for(grads.at[head_span(number), :], g_sem.at[number])
    forward(SELF, True)

    def forward_next(slot, carry):
        @pl.when(slot == SAME_3)
        def _():
            for kind in (KEY, VALUE):
                arrived(SAME_2, kind)
                hand_over(SAME_2, OTHER_2, 2, kind)

        for late in (EXTRA, OTHER_1, OTHER_3, OTHER_2):

            @pl.when(slot == late)
            def _():
                for kind in (KEY, VALUE):
                    arrived(late, kind)

        forward(slot, False)
        return carry

    lax.fori_loop(SELF + 1, SLOTS, forward_next, 0)

    for number in range(group):
        top = tops[number]
        factor = jnp.exp2((top - jnp.max(top, axis=0, keepdims=True)) * exponent)
        total = jnp.sum(factor * sums[number], axis=0, keepdims=True)
        cross = jnp.sum(factor * crosses[number], axis=0, keepdims=True)
        tops[number] = factor / total
        sums[number, 0:1, :] = cross / total

    dq_t[...] = jnp.zeros_like(dq_t)

    def to_owners(slot, kind, number, step, on_core, first):
        for hop in range(first, head_count):
            to, _ = at_head(hop)
            here = pl.ds(pl.multiple_of(to * tokens, tokens), tokens)
            send(
                part.at[slot, kind, here, :], shares.at[number, head, kind],
                part_send.at[slot], share_sem, (to, *at_chip(step, on_core)[1:]),
            )

    def backward(turn, carry):
        slot = SLOTS - 1 - turn
        for number in range(group):
            span = slice(number * rows, (number + 1) * rows)
            probs = scores[slot, number] * tops[number, pl.ds(slot, 1), :]
            p_half[:, span] = probs.astype(jnp.bfloat16)
            ds_half[:, span] = (probs * (pgrads[slot, number] - sums[number, 0:1, :])).astype(
                jnp.bfloat16
            )
        fresh[KEY] = jnp.dot(ds_half[...], queries[...], preferred_element_type=jnp.float32)
        fresh[VALUE] = jnp.dot(p_half[...], grads[...], preferred_element_type=jnp.float32)
        part[slot] = fresh[...].astype(jnp.bfloat16)

        for here, number in ((OTHER_2, 2), (OTHER_3, 1), (OTHER_1, 0)):

            @pl.when(slot == here)
            def _():
                send(
                    part.at[here], part_other.at[number], part_send.at[here],
                    other_sem.at[number], other,
                )

        def add_other(here, kind, number):
            return fresh[kind] + part_other[number, kind].astype(jnp.float32)

        @pl.when(slot == SAME_2)
        def _():
            wait_for(part_other.at[2], other_sem.at[2])
            for kind, to in ((KEY, back_1), (VALUE, next_1)):
                part[SAME_2, kind] = add_other(SAME_2, kind, 2).astype(jnp.bfloat16)
                send(
                    part.at[SAME_2, kind], chain.at[kind], part_send.at[SAME_2],
                    chain_sem.at[kind], to,
                )

        @pl.when(slot == EXTRA)
        def _():
            for kind in (KEY, VALUE):
                to_owners(EXTRA, kind, 2, -4 * (1 - core), 1 - core, 0)

        for here, number, kind, step in ((SAME_3, 1, KEY, -3), (SAME_1, 0, VALUE, -1)):

            @pl.when(slot == here)
            def _():
                wait_for(part_other.at[number], other_sem.at[number])
                part[here, kind] = add_other(here, kind, number).astype(jnp.bfloat16)
                to_owners(here, kind, number, step, core, 0)
                hold[1 - kind] = add_other(here, 1 - kind, number)

        @pl.when(slot == SELF)
        def _():
            for kind in (KEY, VALUE):
                to_owners(SELF, kind, 3, 0, core, 1)
                pltpu.make_async_copy(
                    part.at[SELF, kind, mine, :], shares.at[3, head, kind], share_sem
                ).start()

        dq_t[...] += jnp.dot(keys_t[slot], ds_half[...], preferred_element_type=jnp.float32)
        return carry

    lax.fori_loop(0, SLOTS, backward, 0)

    for slot, kind, number, step in ((SAME_3, VALUE, 1, -3), (SAME_1, KEY, 0, -1)):
        wait_for(chain.at[kind], chain_sem.at[kind])
        part[slot, kind] = (hold[kind] + chain[kind].astype(jnp.float32)).astype(jnp.bfloat16)
        to_owners(slot, kind, number, step, core, 0)

    def send_back(number, carry):
        dq = dq_t[:, head_span(number)].T * score_scale
        dq_half[head_span(number), :] = dq.astype(jnp.bfloat16)
        columns = head_columns(head * group + number)
        for step in range(1, head_count):
            to, device = at_head(step)
            here = pl.ds(pl.multiple_of(number * rows + to * tokens, tokens), tokens)
            send(dq_half.at[here, :], dq_out.at[:, columns], dq_send, dq_sem, device)
        here = pl.ds(pl.multiple_of(number * rows + head * tokens, tokens), tokens)
        pltpu.make_async_copy(dq_half.at[here, :], dq_out.at[:, columns], dq_sem).start()
        return carry

    lax.fori_loop(0, group, send_back, 0)

    peers = head_count - 1
    for kind, (src, kv) in enumerate(((q_in, k_in), (g_in, v_in))):
        wait_for(src.at[:, : peers * group * HEAD_SIZE], qg_send.at[kind])
        wait_for(kv.at[:, : peers * HEAD_SIZE], kv_send.at[kind])
        array = (keys, values)[kind]
        for number in range(4):
            wait_for(array.at[SELF], fwd_send.at[number, kind])
        for number in range(3):
            wait_for(array.at[SELF], fwd_other_send.at[number, kind])
    for slot in range(SELF + 1, SLOTS):
        wait_for(part.at[slot], part_send.at[slot])
    wait_for(part.at[SELF, :, : peers * tokens, :], part_send.at[SELF])
    wait_for(dq_out.at[:, : peers * group * HEAD_SIZE], dq_send)
    wait_for(dq_out, dq_sem)
    wait_for(shares, share_sem)


def finish(dq_in, shares, dq_out, dk_out, dv_out):
    dq_out[...] = dq_in[...]
    heads = shares.shape[1]
    for kind, out in enumerate((dk_out, dv_out)):
        for head in range(heads):
            total = shares[0, head, kind].astype(jnp.float32)
            for number in range(1, SHARES):
                total = total + shares[number, head, kind].astype(jnp.float32)
            if kind == KEY:
                total = total * HEAD_SIZE ** (-0.5)
            out[:, head * HEAD_SIZE : (head + 1) * HEAD_SIZE] = total.astype(jnp.bfloat16)


def body(query_heads, key_heads, value_matrix, out_grad, segment_ids):
    head_count = lax.axis_size("head")
    sizes = (head_count, lax.axis_size("inner"), lax.axis_size("outer"), query_heads.shape[1] // key_heads.shape[1])
    group = sizes[3]
    tokens = query_heads.shape[0]
    rows = head_count * tokens
    half, full = jnp.bfloat16, jnp.float32
    ids = segment_ids.reshape(-1, 128)
    dma = pltpu.SemaphoreType.DMA
    anywhere = pl.BlockSpec(memory_space=pl.ANY)
    dq, shares = pl.pallas_call(
        functools.partial(kernel, sizes),
        out_shape=(
            jax.ShapeDtypeStruct(query_heads.shape, half),
            jax.ShapeDtypeStruct((SHARES, head_count, 2, tokens, HEAD_SIZE), half),
        ),
        in_specs=[anywhere] * 5,
        out_specs=[anywhere] * 2,
        scratch_shapes=[
            pltpu.VMEM(ids.shape, jnp.int32),
            pltpu.VMEM((group * rows, HEAD_SIZE), half),
            pltpu.VMEM((group * rows, HEAD_SIZE), half),
            pltpu.VMEM((SLOTS, rows, HEAD_SIZE), half),
            pltpu.VMEM((SLOTS, rows, HEAD_SIZE), half),
            pltpu.VMEM((SLOTS, HEAD_SIZE, rows), half),
            pltpu.VMEM((SLOTS, rows, KINDS), half),
            pltpu.VMEM((rows, KINDS), half),
            pltpu.VMEM((SLOTS, group, rows, rows), full),
            pltpu.VMEM((SLOTS, group, rows, rows), full),
            pltpu.VMEM((group, SLOTS, rows), full),
            pltpu.VMEM((group, SLOTS, rows), full),
            pltpu.VMEM((group, SLOTS, rows), full),
            pltpu.VMEM((rows, group * rows), half),
            pltpu.VMEM((rows, group * rows), half),
            pltpu.VMEM((HEAD_SIZE, group * rows), full),
            pltpu.VMEM((group * rows, HEAD_SIZE), half),
            pltpu.VMEM((2, rows, HEAD_SIZE), full),
            pltpu.VMEM((2, rows, HEAD_SIZE), full),
            pltpu.VMEM((SLOTS, 2, rows, HEAD_SIZE), half),
            pltpu.VMEM((3, 2, rows, HEAD_SIZE), half),
            pltpu.VMEM((2, rows, HEAD_SIZE), half),
            dma,
            dma((group,)),
            dma((group,)),
            dma((SLOTS, 2)),
            dma((2,)),
            dma((2,)),
            dma((4, 2)),
            dma((3, 2)),
            dma((SLOTS,)),
            dma((3,)),
            dma((2,)),
            dma,
            dma,
            dma,
        ],
        compiler_params=pltpu.CompilerParams(
            collective_id=0, has_side_effects=True, vmem_limit_bytes=56 * 2**20
        ),
    )(query_heads, key_heads, value_matrix, out_grad, ids)
    return pl.pallas_call(
        finish,
        out_shape=(
            jax.ShapeDtypeStruct(query_heads.shape, half),
            jax.ShapeDtypeStruct(key_heads.shape, half),
            jax.ShapeDtypeStruct(value_matrix.shape, half),
        ),
    )(dq, shares)


def solution(mesh):
    split = P(("inner", "outer", "head"), None)
    return jax.shard_map(
        body,
        mesh=mesh,
        in_specs=(split, split, split, split, P()),
        out_specs=(split, split, split),
        check_vma=False,
    )
```

```python
import functools

import jax
import jax.numpy as jnp
from jax import lax
from jax.experimental import pallas as pl
from jax.experimental.pallas import tpu as pltpu
from jax.sharding import PartitionSpec as P

HEAD_SIZE = 128
QUERY_HEADS = 24
KEY_VALUE_HEADS = 4
KINDS = 128
FAR = 1e30
LOG2_E = 1.4426950408889634
MESH = pl.DeviceIdType.MESH
CORES = 2

OTHER_2, OTHER_3, OTHER_1, SELF, SAME_2, EXTRA, SAME_3, SAME_1 = range(8)
SLOTS = 8
CHIPS_BACK = {OTHER_2: 2, SAME_2: 2, OTHER_1: 1, OTHER_3: 3, SAME_3: 3, SAME_1: 1}
SHARES = 4
TOGETHER = 3
KEY, VALUE = range(2)


def kernel(
    sizes,
    q_in, k_in, v_in, g_in, seg_in,
    dq_out, shares,
    seg, queries, grads, keys, values, keys_t, kinds, unkind,
    scores, pgrads, tops, sums, crosses, ds_half, p_half, dq_half,
    fresh, hold, part, part_other, chain,
    seg_sem, q_sem, g_sem, kv_sem, qg_send, kv_send, fwd_send, fwd_other_send,
    part_send, other_sem, chain_sem, share_sem, dq_send, dq_sem,
):
    head_count, inner_count, outer_count, group = sizes
    head = lax.axis_index("head")
    inner = lax.axis_index("inner")
    outer = lax.axis_index("outer")
    core = outer % CORES
    per_inner = outer_count // CORES
    chips = inner_count * per_inner
    chip = inner * per_inner + outer // CORES
    shards = chips * CORES
    place = chip * CORES + core
    tokens = q_in.shape[0]
    rows = head_count * tokens

    def at_chip(step, on_core):
        to = (chip + step + chips) % chips
        return (head, to // per_inner, (to % per_inner) * CORES + on_core)

    def at_head(step):
        to = (head + step) % head_count
        return to, (to, inner, outer)

    def wait_for(ref, sem):
        pltpu.make_async_copy(ref, ref, sem).wait()

    def send(src, dst, send_sem, recv_sem, to):
        pltpu.make_async_remote_copy(
            src_ref=src, dst_ref=dst, send_sem=send_sem, recv_sem=recv_sem,
            device_id=to, device_id_type=MESH,
        ).start()

    other = at_chip(0, 1 - core)
    next_1, next_3 = at_chip(1, core), at_chip(3, core)
    back_1, back_3 = at_chip(-1, core), at_chip(-3, core)
    extra_to = at_chip(4 * core, 1 - core)
    extra_from = at_chip(-4 * (1 - core), 1 - core)

    load_seg = pltpu.make_async_copy(seg_in, seg, seg_sem)
    load_seg.start()

    barrier = pltpu.get_barrier_semaphore()
    partners = [at_head(step)[1] for step in range(1, head_count)]
    partners += [other, next_1, next_3, back_1, back_3]
    far = at_chip(8 * core - 4, 1 - core)
    for partner in partners + [far]:
        pl.semaphore_signal(barrier, inc=1, device_id=partner, device_id_type=MESH)
    pl.semaphore_wait(barrier, len(partners) + 1)

    mine = pl.ds(pl.multiple_of(head * tokens, tokens), tokens)

    def head_columns(number):
        return pl.ds(pl.multiple_of(number * HEAD_SIZE, HEAD_SIZE), HEAD_SIZE)

    for kind, (src, dst) in enumerate(((k_in, keys), (v_in, values))):
        for step in range(1, head_count):
            to, device = at_head(step)
            send(
                src.at[:, head_columns(to)], dst.at[SELF, mine, :],
                kv_send.at[kind], kv_sem.at[SELF, kind], device,
            )
        pltpu.make_async_copy(
            src.at[:, head_columns(head)], dst.at[SELF, mine, :], kv_sem.at[SELF, kind]
        ).start()

    def send_head(number, carry):
        target = pl.ds(pl.multiple_of(number * rows + head * tokens, tokens), tokens)
        for kind, (src, dst, sem) in enumerate(
            ((q_in, queries, q_sem), (g_in, grads, g_sem))
        ):
            for step in range(1, head_count):
                to, device = at_head(step)
                send(
                    src.at[:, head_columns(to * group + number)], dst.at[target, :],
                    qg_send.at[kind], sem.at[number], device,
                )
            pltpu.make_async_copy(
                src.at[:, head_columns(head * group + number)], dst.at[target, :], sem.at[number]
            ).start()
        return carry

    lax.fori_loop(0, group, send_head, 0)

    load_seg.wait()
    lanes = seg.shape[1]
    seg_rows = rows // lanes
    session = lax.broadcasted_iota(jnp.int32, (KINDS, lanes), 0)

    def shard_of(slot):
        if slot == SELF:
            return place
        if slot == EXTRA:
            return (place - 7 + 6 * core + shards) % shards
        on_core = core if slot in (SAME_1, SAME_2, SAME_3) else 1 - core
        return ((chip - CHIPS_BACK[slot] + chips) % chips) * CORES + on_core

    for slot in range(SLOTS):
        for part_row in range(seg_rows):
            ids = seg[pl.ds(shard_of(slot) * seg_rows + part_row, 1), :]
            ones = jnp.where(session == ids, 1.0, 0.0).astype(jnp.float32).T
            span = slice(part_row * lanes, (part_row + 1) * lanes)
            kinds[slot, span, :] = ones.astype(jnp.bfloat16)
            if slot == SELF:
                unkind[span, :] = ((ones - 1.0) * FAR).astype(jnp.bfloat16)

    both = ((KEY, keys), (VALUE, values))
    onward = {SAME_1: (0, next_1), SAME_3: (1, next_3), EXTRA: (2, extra_to)}

    def pass_on(slot, kind):
        number, to = onward[slot]
        array = both[kind][1]
        send(
            array.at[SELF], array.at[slot],
            fwd_send.at[number, kind], kv_sem.at[slot, kind], to,
        )

    def arrived(slot, kind):
        wait_for(both[kind][1].at[slot], kv_sem.at[slot, kind])

    arrived(SELF, KEY)
    pass_on(SAME_1, KEY)
    arrived(SELF, VALUE)
    pass_on(SAME_3, VALUE)
    pass_on(SAME_1, VALUE)
    pass_on(SAME_3, KEY)
    pass_on(EXTRA, KEY)
    pass_on(EXTRA, VALUE)

    def hand_over(slot, slot_there, number, kind):
        array = both[kind][1]
        send(
            array.at[slot], array.at[slot_there],
            fwd_other_send.at[number, kind], kv_sem.at[slot_there, kind], other,
        )

    def relay(slot, kind, to):
        array = both[kind][1]
        send(
            array.at[slot], array.at[SAME_2], fwd_send.at[3, kind], kv_sem.at[SAME_2, kind], to
        )

    score_scale = HEAD_SIZE ** (-0.5)
    exponent = score_scale * LOG2_E
    over_last = (((1,), (1,)), ((), ()))

    def folded(block):
        return block.reshape(rows // 8, 8, block.shape[1])

    def head_span(number):
        return pl.ds(pl.multiple_of(number * rows, rows), rows)

    def turn_keys(slot):
        turned = keys[slot].astype(jnp.float32).T.astype(jnp.bfloat16)
        if isinstance(slot, int):
            keys_t[:, slot * rows : (slot + 1) * rows] = turned
        else:
            keys_t[:, head_span(slot)] = turned

    def forward(slot, heads, masked):
        wide_keys = jnp.concatenate([keys[slot], kinds[slot]], axis=1)
        here = pl.ds(slot, 1)
        for first in range(heads.start, heads.stop, TOGETHER):
            count = min(TOGETHER, heads.stop - first)
            span = slice(first * rows, (first + count) * rows)
            wide_queries = jnp.concatenate(
                [queries[span, :], jnp.concatenate([unkind[...]] * count, axis=0)], axis=1
            )
            block = lax.dot_general(
                wide_keys, wide_queries, over_last, preferred_element_type=jnp.float32
            )
            if masked:
                key_row = lax.broadcasted_iota(jnp.int32, (rows, rows), 0)
                query_column = lax.broadcasted_iota(jnp.int32, (rows, rows), 1)
                earlier = jnp.concatenate([key_row <= query_column] * count, axis=1)
                block = jnp.where(earlier, block, -FAR)
            slopes = lax.dot_general(
                values[slot], grads[span, :], over_last, preferred_element_type=jnp.float32
            )
            top = jnp.max(jnp.max(folded(block), axis=0), axis=0, keepdims=True)
            weights = jnp.exp2((block - top) * exponent)
            scores[slot, :, span] = weights
            pgrads[slot, :, span] = slopes
            tops[here, span] = top
            sums[here, span] = jnp.sum(jnp.sum(folded(weights), axis=0), axis=0, keepdims=True)
            crosses[here, span] = jnp.sum(
                jnp.sum(folded(weights * slopes), axis=0), axis=0, keepdims=True
            )

    def own_block(heads):
        for number in heads:
            wait_for(queries.at[head_span(number), :], q_sem.at[number])
            wait_for(grads.at[head_span(number), :], g_sem.at[number])
            forward(SELF, range(number, number + 1), True)

    turn_keys(SELF)
    own_block(range(0, group // 2))
    arrived(SAME_1, KEY)
    relay(SAME_1, KEY, next_1)
    hand_over(SAME_1, OTHER_1, 0, KEY)
    arrived(SAME_3, VALUE)
    relay(SAME_3, VALUE, back_1)
    hand_over(SAME_3, OTHER_3, 1, VALUE)
    own_block(range(group // 2, group - 1))
    arrived(SAME_1, VALUE)
    hand_over(SAME_1, OTHER_1, 0, VALUE)
    arrived(SAME_3, KEY)
    hand_over(SAME_3, OTHER_3, 1, KEY)
    own_block(range(group - 1, group))

    def forward_next(turn, carry):
        slot = SLOTS - 1 - turn - turn // 4

        @pl.when(slot == SAME_3)
        def _():
            for kind in (KEY, VALUE):
                arrived(SAME_2, kind)
                hand_over(SAME_2, OTHER_2, 2, kind)

        for late in (EXTRA, OTHER_1, OTHER_3, OTHER_2):

            @pl.when(slot == late)
            def _():
                for kind in (KEY, VALUE):
                    arrived(late, kind)

        turn_keys(slot)
        forward(slot, range(group), False)
        return carry

    lax.fori_loop(0, SLOTS - 1, forward_next, 0)

    top = tops[...]
    factor = jnp.exp2((top - jnp.max(top, axis=0, keepdims=True)) * exponent)
    total = jnp.sum(factor * sums[...], axis=0, keepdims=True)
    cross = jnp.sum(factor * crosses[...], axis=0, keepdims=True)
    tops[...] = factor / total
    sums[0:1, :] = cross / total

    def to_owners(slot, kind, number, step, on_core, first):
        for hop in range(first, head_count):
            to, _ = at_head(hop)
            here = pl.ds(pl.multiple_of(to * tokens, tokens), tokens)
            send(
                part.at[slot, kind, here, :], shares.at[number, head, kind],
                part_send.at[slot], share_sem, (to, *at_chip(step, on_core)[1:]),
            )

    def backward(slot, carry):
        for first in range(0, group, TOGETHER):
            span = slice(first * rows, min(first + TOGETHER, group) * rows)
            probs = scores[slot, :, span] * tops[pl.ds(slot, 1), span]
            p_half[:, span] = probs.astype(jnp.bfloat16)
            ds_half[slot, :, span] = (probs * (pgrads[slot, :, span] - sums[0:1, span])).astype(
                jnp.bfloat16
            )
        fresh[KEY] = jnp.dot(ds_half[slot], queries[...], preferred_element_type=jnp.float32)
        fresh[VALUE] = jnp.dot(p_half[...], grads[...], preferred_element_type=jnp.float32)
        part[slot] = fresh[...].astype(jnp.bfloat16)

        for here, number in ((OTHER_2, 2), (OTHER_3, 1), (OTHER_1, 0)):

            @pl.when(slot == here)
            def _():
                send(
                    part.at[here], part_other.at[number], part_send.at[here],
                    other_sem.at[number], other,
                )

        def add_other(here, kind, number):
            return fresh[kind] + part_other[number, kind].astype(jnp.float32)

        @pl.when(slot == SAME_2)
        def _():
            wait_for(part_other.at[2], other_sem.at[2])
            for kind, to in ((KEY, back_1), (VALUE, next_1)):
                part[SAME_2, kind] = add_other(SAME_2, kind, 2).astype(jnp.bfloat16)
                send(
                    part.at[SAME_2, kind], chain.at[kind], part_send.at[SAME_2],
                    chain_sem.at[kind], to,
                )

        @pl.when(slot == EXTRA)
        def _():
            for kind in (KEY, VALUE):
                to_owners(EXTRA, kind, 2, -4 * (1 - core), 1 - core, 0)

        for here, number, kind, step in ((SAME_3, 1, KEY, -3), (SAME_1, 0, VALUE, -1)):

            @pl.when(slot == here)
            def _():
                wait_for(part_other.at[number], other_sem.at[number])
                part[here, kind] = add_other(here, kind, number).astype(jnp.bfloat16)
                to_owners(here, kind, number, step, core, 0)
                hold[1 - kind] = add_other(here, 1 - kind, number)

        @pl.when(slot == SELF)
        def _():
            for kind in (KEY, VALUE):
                to_owners(SELF, kind, 3, 0, core, 1)
                pltpu.make_async_copy(
                    part.at[SELF, kind, mine, :], shares.at[3, head, kind], share_sem
                ).start()

        return carry

    lax.fori_loop(0, SLOTS, backward, 0)

    def send_back(number, carry):
        blocks = ds_half[:, :, head_span(number)].reshape(SLOTS * rows, rows)
        dq = jnp.dot(keys_t[...], blocks, preferred_element_type=jnp.float32).T * score_scale
        dq_half[head_span(number), :] = dq.astype(jnp.bfloat16)
        columns = head_columns(head * group + number)
        for step in range(1, head_count):
            to, device = at_head(step)
            here = pl.ds(pl.multiple_of(number * rows + to * tokens, tokens), tokens)
            send(dq_half.at[here, :], dq_out.at[:, columns], dq_send, dq_sem, device)
        here = pl.ds(pl.multiple_of(number * rows + head * tokens, tokens), tokens)
        pltpu.make_async_copy(dq_half.at[here, :], dq_out.at[:, columns], dq_sem).start()
        return carry

    lax.fori_loop(0, group, send_back, 0)

    for slot, kind, number, step in ((SAME_3, VALUE, 1, -3), (SAME_1, KEY, 0, -1)):
        wait_for(chain.at[kind], chain_sem.at[kind])
        part[slot, kind] = (hold[kind] + chain[kind].astype(jnp.float32)).astype(jnp.bfloat16)
        to_owners(slot, kind, number, step, core, 0)

    peers = head_count - 1
    for kind, (src, kv) in enumerate(((q_in, k_in), (g_in, v_in))):
        wait_for(src.at[:, : peers * group * HEAD_SIZE], qg_send.at[kind])
        wait_for(kv.at[:, : peers * HEAD_SIZE], kv_send.at[kind])
        array = (keys, values)[kind]
        for number in range(4):
            wait_for(array.at[SELF], fwd_send.at[number, kind])
        for number in range(3):
            wait_for(array.at[SELF], fwd_other_send.at[number, kind])
    for slot in range(SLOTS):
        if slot != SELF:
            wait_for(part.at[slot], part_send.at[slot])
    wait_for(part.at[SELF, :, : peers * tokens, :], part_send.at[SELF])
    wait_for(dq_out.at[:, : peers * group * HEAD_SIZE], dq_send)
    wait_for(dq_out, dq_sem)
    wait_for(shares, share_sem)


def finish(dq_in, shares, dq_out, dk_out, dv_out):
    dq_out[...] = dq_in[...]
    heads = shares.shape[1]
    for kind, out in enumerate((dk_out, dv_out)):
        for head in range(heads):
            total = shares[0, head, kind].astype(jnp.float32)
            for number in range(1, SHARES):
                total = total + shares[number, head, kind].astype(jnp.float32)
            if kind == KEY:
                total = total * HEAD_SIZE ** (-0.5)
            out[:, head * HEAD_SIZE : (head + 1) * HEAD_SIZE] = total.astype(jnp.bfloat16)


def body(query_heads, key_heads, value_matrix, out_grad, segment_ids):
    head_count = lax.axis_size("head")
    sizes = (head_count, lax.axis_size("inner"), lax.axis_size("outer"), query_heads.shape[1] // key_heads.shape[1])
    group = sizes[3]
    tokens = query_heads.shape[0]
    rows = head_count * tokens
    half, full = jnp.bfloat16, jnp.float32
    ids = segment_ids.reshape(-1, 128)
    dma = pltpu.SemaphoreType.DMA
    anywhere = pl.BlockSpec(memory_space=pl.ANY)
    dq, shares = pl.pallas_call(
        functools.partial(kernel, sizes),
        out_shape=(
            jax.ShapeDtypeStruct(query_heads.shape, half),
            jax.ShapeDtypeStruct((SHARES, head_count, 2, tokens, HEAD_SIZE), half),
        ),
        in_specs=[anywhere] * 5,
        out_specs=[anywhere] * 2,
        scratch_shapes=[
            pltpu.VMEM(ids.shape, jnp.int32),
            pltpu.VMEM((group * rows, HEAD_SIZE), half),
            pltpu.VMEM((group * rows, HEAD_SIZE), half),
            pltpu.VMEM((SLOTS, rows, HEAD_SIZE), half),
            pltpu.VMEM((SLOTS, rows, HEAD_SIZE), half),
            pltpu.VMEM((HEAD_SIZE, SLOTS * rows), half),
            pltpu.VMEM((SLOTS, rows, KINDS), half),
            pltpu.VMEM((rows, KINDS), half),
            pltpu.VMEM((SLOTS, rows, group * rows), full),
            pltpu.VMEM((SLOTS, rows, group * rows), full),
            pltpu.VMEM((SLOTS, group * rows), full),
            pltpu.VMEM((SLOTS, group * rows), full),
            pltpu.VMEM((SLOTS, group * rows), full),
            pltpu.VMEM((SLOTS, rows, group * rows), half),
            pltpu.VMEM((rows, group * rows), half),
            pltpu.VMEM((group * rows, HEAD_SIZE), half),
            pltpu.VMEM((2, rows, HEAD_SIZE), full),
            pltpu.VMEM((2, rows, HEAD_SIZE), full),
            pltpu.VMEM((SLOTS, 2, rows, HEAD_SIZE), half),
            pltpu.VMEM((3, 2, rows, HEAD_SIZE), half),
            pltpu.VMEM((2, rows, HEAD_SIZE), half),
            dma,
            dma((group,)),
            dma((group,)),
            dma((SLOTS, 2)),
            dma((2,)),
            dma((2,)),
            dma((4, 2)),
            dma((3, 2)),
            dma((SLOTS,)),
            dma((3,)),
            dma((2,)),
            dma,
            dma,
            dma,
        ],
        compiler_params=pltpu.CompilerParams(
            collective_id=0, has_side_effects=True, vmem_limit_bytes=56 * 2**20
        ),
    )(query_heads, key_heads, value_matrix, out_grad, ids)
    return pl.pallas_call(
        finish,
        out_shape=(
            jax.ShapeDtypeStruct(query_heads.shape, half),
            jax.ShapeDtypeStruct(key_heads.shape, half),
            jax.ShapeDtypeStruct(value_matrix.shape, half),
        ),
    )(dq, shares)


def solution(mesh):
    split = P(("inner", "outer", "head"), None)
    return jax.shard_map(
        body,
        mesh=mesh,
        in_specs=(split, split, split, split, P()),
        out_specs=(split, split, split),
        check_vma=False,
    )
```

```python
import functools

import jax
import jax.numpy as jnp
from jax import lax
from jax.experimental import pallas as pl
from jax.experimental.pallas import tpu as pltpu
from jax.sharding import PartitionSpec as P

HEAD_SIZE = 128
QUERY_HEADS = 24
KEY_VALUE_HEADS = 4
KINDS = 128
FAR = 1e30
LOG2_E = 1.4426950408889634
MESH = pl.DeviceIdType.MESH
CORES = 2

OTHER_2, OTHER_3, OTHER_1, SELF, SAME_2, EXTRA, SAME_3, SAME_1 = range(8)
SLOTS = 8
CHIPS_BACK = {OTHER_2: 2, SAME_2: 2, OTHER_1: 1, OTHER_3: 3, SAME_3: 3, SAME_1: 1}
SHARES = 4
TOGETHER = 3
KEY, VALUE = range(2)


def kernel(
    sizes,
    q_in, k_in, v_in, g_in, seg_in,
    dq_out, shares,
    seg, queries, grads, keys, values, keys_t, kinds, unkind,
    scores, pgrads, tops, sums, crosses, ds_half, p_half, dq_half,
    fresh, hold, part, part_other, chain,
    seg_sem, q_sem, g_sem, kv_sem, qg_send, kv_send, fwd_send, fwd_other_send,
    part_send, other_sem, chain_sem, share_sem, dq_send, dq_sem,
):
    head_count, inner_count, outer_count, group = sizes
    head = lax.axis_index("head")
    inner = lax.axis_index("inner")
    outer = lax.axis_index("outer")
    core = outer % CORES
    per_inner = outer_count // CORES
    chips = inner_count * per_inner
    chip = inner * per_inner + outer // CORES
    shards = chips * CORES
    place = chip * CORES + core
    tokens = q_in.shape[0]
    rows = head_count * tokens

    def at_chip(step, on_core):
        to = (chip + step + chips) % chips
        return (head, to // per_inner, (to % per_inner) * CORES + on_core)

    def at_head(step):
        to = (head + step) % head_count
        return to, (to, inner, outer)

    def wait_for(ref, sem):
        pltpu.make_async_copy(ref, ref, sem).wait()

    def send(src, dst, send_sem, recv_sem, to):
        pltpu.make_async_remote_copy(
            src_ref=src, dst_ref=dst, send_sem=send_sem, recv_sem=recv_sem,
            device_id=to, device_id_type=MESH,
        ).start()

    other = at_chip(0, 1 - core)
    next_1, next_3 = at_chip(1, core), at_chip(3, core)
    back_1, back_3 = at_chip(-1, core), at_chip(-3, core)
    extra_to = at_chip(4 * core, 1 - core)
    extra_from = at_chip(-4 * (1 - core), 1 - core)

    load_seg = pltpu.make_async_copy(seg_in, seg, seg_sem)
    load_seg.start()

    barrier = pltpu.get_barrier_semaphore()
    partners = [at_head(step)[1] for step in range(1, head_count)]
    partners += [other, next_1, next_3, back_1, back_3]
    far = at_chip(8 * core - 4, 1 - core)
    for partner in partners + [far]:
        pl.semaphore_signal(barrier, inc=1, device_id=partner, device_id_type=MESH)
    pl.semaphore_wait(barrier, len(partners) + 1)

    mine = pl.ds(pl.multiple_of(head * tokens, tokens), tokens)

    def head_columns(number):
        return pl.ds(pl.multiple_of(number * HEAD_SIZE, HEAD_SIZE), HEAD_SIZE)

    for kind, (src, dst) in enumerate(((k_in, keys), (v_in, values))):
        for step in range(1, head_count):
            to, device = at_head(step)
            send(
                src.at[:, head_columns(to)], dst.at[SELF, mine, :],
                kv_send.at[kind], kv_sem.at[SELF, kind], device,
            )
        pltpu.make_async_copy(
            src.at[:, head_columns(head)], dst.at[SELF, mine, :], kv_sem.at[SELF, kind]
        ).start()

    def send_head(number, carry):
        target = pl.ds(pl.multiple_of(number * rows + head * tokens, tokens), tokens)
        for kind, (src, dst, sem) in enumerate(
            ((q_in, queries, q_sem), (g_in, grads, g_sem))
        ):
            for step in range(1, head_count):
                to, device = at_head(step)
                send(
                    src.at[:, head_columns(to * group + number)], dst.at[target, :],
                    qg_send.at[kind], sem.at[number], device,
                )
            pltpu.make_async_copy(
                src.at[:, head_columns(head * group + number)], dst.at[target, :], sem.at[number]
            ).start()
        return carry

    lax.fori_loop(0, group, send_head, 0)

    load_seg.wait()
    lanes = seg.shape[1]
    seg_rows = rows // lanes
    session = lax.broadcasted_iota(jnp.int32, (KINDS, lanes), 0)

    def shard_of(slot):
        if slot == SELF:
            return place
        if slot == EXTRA:
            return (place - 7 + 6 * core + shards) % shards
        on_core = core if slot in (SAME_1, SAME_2, SAME_3) else 1 - core
        return ((chip - CHIPS_BACK[slot] + chips) % chips) * CORES + on_core

    for slot in range(SLOTS):
        for part_row in range(seg_rows):
            ids = seg[pl.ds(shard_of(slot) * seg_rows + part_row, 1), :]
            ones = jnp.where(session == ids, 1.0, 0.0).astype(jnp.float32).T
            span = slice(part_row * lanes, (part_row + 1) * lanes)
            kinds[slot, span, :] = ones.astype(jnp.bfloat16)
            if slot == SELF:
                unkind[span, :] = ((ones - 1.0) * FAR).astype(jnp.bfloat16)

    both = ((KEY, keys), (VALUE, values))
    onward = {SAME_1: (0, next_1), SAME_3: (1, next_3), EXTRA: (2, extra_to)}

    def pass_on(slot, kind):
        number, to = onward[slot]
        array = both[kind][1]
        send(
            array.at[SELF], array.at[slot],
            fwd_send.at[number, kind], kv_sem.at[slot, kind], to,
        )

    def arrived(slot, kind):
        wait_for(both[kind][1].at[slot], kv_sem.at[slot, kind])

    arrived(SELF, KEY)
    pass_on(SAME_1, KEY)
    arrived(SELF, VALUE)
    pass_on(SAME_3, VALUE)
    pass_on(SAME_1, VALUE)
    pass_on(SAME_3, KEY)
    pass_on(EXTRA, KEY)
    pass_on(EXTRA, VALUE)

    def hand_over(slot, slot_there, number, kind):
        array = both[kind][1]
        send(
            array.at[slot], array.at[slot_there],
            fwd_other_send.at[number, kind], kv_sem.at[slot_there, kind], other,
        )

    def relay(slot, kind, to):
        array = both[kind][1]
        send(
            array.at[slot], array.at[SAME_2], fwd_send.at[3, kind], kv_sem.at[SAME_2, kind], to
        )

    score_scale = HEAD_SIZE ** (-0.5)
    exponent = score_scale * LOG2_E
    over_last = (((1,), (1,)), ((), ()))

    def folded(block):
        return block.reshape(rows // 8, 8, block.shape[1])

    def head_span(number):
        return pl.ds(pl.multiple_of(number * rows, rows), rows)

    def turn_keys(slot):
        turned = keys[slot].astype(jnp.float32).T.astype(jnp.bfloat16)
        if isinstance(slot, int):
            keys_t[:, slot * rows : (slot + 1) * rows] = turned
        else:
            keys_t[:, head_span(slot)] = turned

    def forward(slot, heads, masked):
        wide_keys = jnp.concatenate([keys[slot], kinds[slot]], axis=1)
        here = pl.ds(slot, 1)
        for first in range(heads.start, heads.stop, TOGETHER):
            count = min(TOGETHER, heads.stop - first)
            span = slice(first * rows, (first + count) * rows)
            wide_queries = jnp.concatenate(
                [queries[span, :], jnp.concatenate([unkind[...]] * count, axis=0)], axis=1
            )
            block = lax.dot_general(
                wide_keys, wide_queries, over_last, preferred_element_type=jnp.float32
            )
            if masked:
                key_row = lax.broadcasted_iota(jnp.int32, (rows, rows), 0)
                query_column = lax.broadcasted_iota(jnp.int32, (rows, rows), 1)
                earlier = jnp.concatenate([key_row <= query_column] * count, axis=1)
                block = jnp.where(earlier, block, -FAR)
            slopes = lax.dot_general(
                values[slot], grads[span, :], over_last, preferred_element_type=jnp.float32
            )
            top = jnp.max(jnp.max(folded(block), axis=0), axis=0, keepdims=True)
            weights = jnp.exp2((block - top) * exponent)
            scores[slot, :, span] = weights
            pgrads[slot, :, span] = slopes
            tops[here, span] = top
            sums[here, span] = jnp.sum(jnp.sum(folded(weights), axis=0), axis=0, keepdims=True)
            crosses[here, span] = jnp.sum(
                jnp.sum(folded(weights * slopes), axis=0), axis=0, keepdims=True
            )

    def own_block(heads):
        for number in heads:
            wait_for(queries.at[head_span(number), :], q_sem.at[number])
            wait_for(grads.at[head_span(number), :], g_sem.at[number])
            forward(SELF, range(number, number + 1), True)

    turn_keys(SELF)
    own_block(range(0, group // 2))
    arrived(SAME_1, KEY)
    relay(SAME_1, KEY, next_1)
    hand_over(SAME_1, OTHER_1, 0, KEY)
    arrived(SAME_3, VALUE)
    relay(SAME_3, VALUE, back_1)
    hand_over(SAME_3, OTHER_3, 1, VALUE)
    own_block(range(group // 2, group - 1))
    arrived(SAME_1, VALUE)
    hand_over(SAME_1, OTHER_1, 0, VALUE)
    arrived(SAME_3, KEY)
    hand_over(SAME_3, OTHER_3, 1, KEY)
    own_block(range(group - 1, group))

    def forward_next(turn, carry):
        slot = SLOTS - 1 - turn - turn // 4

        @pl.when(slot == EXTRA)
        def _():
            for kind in (KEY, VALUE):
                arrived(SAME_2, kind)
                hand_over(SAME_2, OTHER_2, 2, kind)

        for late in (EXTRA, OTHER_1, OTHER_3, OTHER_2):

            @pl.when(slot == late)
            def _():
                for kind in (KEY, VALUE):
                    arrived(late, kind)

        turn_keys(slot)
        forward(slot, range(group), False)
        return carry

    lax.fori_loop(0, SLOTS - 1, forward_next, 0)

    top = tops[...]
    factor = jnp.exp2((top - jnp.max(top, axis=0, keepdims=True)) * exponent)
    total = jnp.sum(factor * sums[...], axis=0, keepdims=True)
    cross = jnp.sum(factor * crosses[...], axis=0, keepdims=True)
    tops[...] = factor / total
    sums[0:1, :] = cross / total

    def to_owners(slot, kind, number, step, on_core, first):
        for hop in range(first, head_count):
            to, _ = at_head(hop)
            here = pl.ds(pl.multiple_of(to * tokens, tokens), tokens)
            send(
                part.at[slot, kind, here, :], shares.at[number, head, kind],
                part_send.at[slot], share_sem, (to, *at_chip(step, on_core)[1:]),
            )

    def only(condition):
        return (lambda work: work()) if condition else (lambda work: None)

    def backward(slot):
        for first in range(0, group, TOGETHER):
            span = slice(first * rows, min(first + TOGETHER, group) * rows)
            probs = scores[slot, :, span] * tops[pl.ds(slot, 1), span]
            p_half[:, span] = probs.astype(jnp.bfloat16)
            ds_half[slot, :, span] = (probs * (pgrads[slot, :, span] - sums[0:1, span])).astype(
                jnp.bfloat16
            )
        fresh[KEY] = jnp.dot(ds_half[slot], queries[...], preferred_element_type=jnp.float32)
        fresh[VALUE] = jnp.dot(p_half[...], grads[...], preferred_element_type=jnp.float32)
        part[slot] = fresh[...].astype(jnp.bfloat16)

        for here, number in ((OTHER_2, 2), (OTHER_3, 1), (OTHER_1, 0)):

            @only(slot == here)
            def _():
                send(
                    part.at[here], part_other.at[number], part_send.at[here],
                    other_sem.at[number], other,
                )

        def add_other(here, kind, number):
            return fresh[kind] + part_other[number, kind].astype(jnp.float32)

        @only(slot == SAME_2)
        def _():
            wait_for(part_other.at[2], other_sem.at[2])
            for kind, to in ((KEY, back_1), (VALUE, next_1)):
                part[SAME_2, kind] = add_other(SAME_2, kind, 2).astype(jnp.bfloat16)
                send(
                    part.at[SAME_2, kind], chain.at[kind], part_send.at[SAME_2],
                    chain_sem.at[kind], to,
                )

        @only(slot == EXTRA)
        def _():
            for kind in (KEY, VALUE):
                to_owners(EXTRA, kind, 2, -4 * (1 - core), 1 - core, 0)

        for here, number, kind, step in ((SAME_3, 1, KEY, -3), (SAME_1, 0, VALUE, -1)):

            @only(slot == here)
            def _():
                wait_for(part_other.at[number], other_sem.at[number])
                part[here, kind] = add_other(here, kind, number).astype(jnp.bfloat16)
                to_owners(here, kind, number, step, core, 0)
                hold[1 - kind] = add_other(here, 1 - kind, number)

        @only(slot == SELF)
        def _():
            for kind in (KEY, VALUE):
                to_owners(SELF, kind, 3, 0, core, 1)
                pltpu.make_async_copy(
                    part.at[SELF, kind, mine, :], shares.at[3, head, kind], share_sem
                ).start()


    for slot in (OTHER_2, OTHER_3, OTHER_1, SAME_2, SELF, EXTRA, SAME_3, SAME_1):
        backward(slot)

    def send_back(number, carry):
        blocks = ds_half[:, :, head_span(number)].reshape(SLOTS * rows, rows)
        dq = jnp.dot(keys_t[...], blocks, preferred_element_type=jnp.float32).T * score_scale
        dq_half[head_span(number), :] = dq.astype(jnp.bfloat16)
        columns = head_columns(head * group + number)
        for step in range(1, head_count):
            to, device = at_head(step)
            here = pl.ds(pl.multiple_of(number * rows + to * tokens, tokens), tokens)
            send(dq_half.at[here, :], dq_out.at[:, columns], dq_send, dq_sem, device)
        here = pl.ds(pl.multiple_of(number * rows + head * tokens, tokens), tokens)
        pltpu.make_async_copy(dq_half.at[here, :], dq_out.at[:, columns], dq_sem).start()
        return carry

    def send_some(turn, carry):
        for one in range(3):
            send_back(turn * 3 + one, carry)
        return carry

    lax.fori_loop(0, group // 3, send_some, 0)

    for slot, kind, number, step in ((SAME_3, VALUE, 1, -3), (SAME_1, KEY, 0, -1)):
        wait_for(chain.at[kind], chain_sem.at[kind])
        part[slot, kind] = (hold[kind] + chain[kind].astype(jnp.float32)).astype(jnp.bfloat16)
        to_owners(slot, kind, number, step, core, 0)

    peers = head_count - 1
    for kind, (src, kv) in enumerate(((q_in, k_in), (g_in, v_in))):
        wait_for(src.at[:, : peers * group * HEAD_SIZE], qg_send.at[kind])
        wait_for(kv.at[:, : peers * HEAD_SIZE], kv_send.at[kind])
        array = (keys, values)[kind]
        for number in range(4):
            wait_for(array.at[SELF], fwd_send.at[number, kind])
        for number in range(3):
            wait_for(array.at[SELF], fwd_other_send.at[number, kind])
    for slot in range(SLOTS):
        if slot != SELF:
            wait_for(part.at[slot], part_send.at[slot])
    wait_for(part.at[SELF, :, : peers * tokens, :], part_send.at[SELF])
    wait_for(dq_out.at[:, : peers * group * HEAD_SIZE], dq_send)
    wait_for(dq_out, dq_sem)
    wait_for(shares, share_sem)


def finish(dq_in, shares, dq_out, dk_out, dv_out):
    dq_out[...] = dq_in[...]
    heads = shares.shape[1]
    for kind, out in enumerate((dk_out, dv_out)):
        for head in range(heads):
            total = shares[0, head, kind].astype(jnp.float32)
            for number in range(1, SHARES):
                total = total + shares[number, head, kind].astype(jnp.float32)
            if kind == KEY:
                total = total * HEAD_SIZE ** (-0.5)
            out[:, head * HEAD_SIZE : (head + 1) * HEAD_SIZE] = total.astype(jnp.bfloat16)


def body(query_heads, key_heads, value_matrix, out_grad, segment_ids):
    head_count = lax.axis_size("head")
    sizes = (head_count, lax.axis_size("inner"), lax.axis_size("outer"), query_heads.shape[1] // key_heads.shape[1])
    group = sizes[3]
    tokens = query_heads.shape[0]
    rows = head_count * tokens
    half, full = jnp.bfloat16, jnp.float32
    ids = segment_ids.reshape(-1, 128)
    dma = pltpu.SemaphoreType.DMA
    anywhere = pl.BlockSpec(memory_space=pl.ANY)
    dq, shares = pl.pallas_call(
        functools.partial(kernel, sizes),
        out_shape=(
            jax.ShapeDtypeStruct(query_heads.shape, half),
            jax.ShapeDtypeStruct((SHARES, head_count, 2, tokens, HEAD_SIZE), half),
        ),
        in_specs=[anywhere] * 5,
        out_specs=[anywhere] * 2,
        scratch_shapes=[
            pltpu.VMEM(ids.shape, jnp.int32),
            pltpu.VMEM((group * rows, HEAD_SIZE), half),
            pltpu.VMEM((group * rows, HEAD_SIZE), half),
            pltpu.VMEM((SLOTS, rows, HEAD_SIZE), half),
            pltpu.VMEM((SLOTS, rows, HEAD_SIZE), half),
            pltpu.VMEM((HEAD_SIZE, SLOTS * rows), half),
            pltpu.VMEM((SLOTS, rows, KINDS), half),
            pltpu.VMEM((rows, KINDS), half),
            pltpu.VMEM((SLOTS, rows, group * rows), full),
            pltpu.VMEM((SLOTS, rows, group * rows), full),
            pltpu.VMEM((SLOTS, group * rows), full),
            pltpu.VMEM((SLOTS, group * rows), full),
            pltpu.VMEM((SLOTS, group * rows), full),
            pltpu.VMEM((SLOTS, rows, group * rows), half),
            pltpu.VMEM((rows, group * rows), half),
            pltpu.VMEM((group * rows, HEAD_SIZE), half),
            pltpu.VMEM((2, rows, HEAD_SIZE), full),
            pltpu.VMEM((2, rows, HEAD_SIZE), full),
            pltpu.VMEM((SLOTS, 2, rows, HEAD_SIZE), half),
            pltpu.VMEM((3, 2, rows, HEAD_SIZE), half),
            pltpu.VMEM((2, rows, HEAD_SIZE), half),
            dma,
            dma((group,)),
            dma((group,)),
            dma((SLOTS, 2)),
            dma((2,)),
            dma((2,)),
            dma((4, 2)),
            dma((3, 2)),
            dma((SLOTS,)),
            dma((3,)),
            dma((2,)),
            dma,
            dma,
            dma,
        ],
        compiler_params=pltpu.CompilerParams(
            collective_id=0, has_side_effects=True, vmem_limit_bytes=56 * 2**20
        ),
    )(query_heads, key_heads, value_matrix, out_grad, ids)
    return pl.pallas_call(
        finish,
        out_shape=(
            jax.ShapeDtypeStruct(query_heads.shape, half),
            jax.ShapeDtypeStruct(key_heads.shape, half),
            jax.ShapeDtypeStruct(value_matrix.shape, half),
        ),
    )(dq, shares)


def solution(mesh):
    split = P(("inner", "outer", "head"), None)
    return jax.shard_map(
        body,
        mesh=mesh,
        in_specs=(split, split, split, split, P()),
        out_specs=(split, split, split),
        check_vma=False,
    )
```

```python
import functools

import jax
import jax.numpy as jnp
from jax import lax
from jax.experimental import pallas as pl
from jax.experimental.pallas import tpu as pltpu
from jax.sharding import PartitionSpec as P

HEAD_SIZE = 128
QUERY_HEADS = 24
KEY_VALUE_HEADS = 4
KINDS = 128
FAR = 1e30
LOG2_E = 1.4426950408889634
MESH = pl.DeviceIdType.MESH
CORES = 2

OTHER_2, OTHER_3, OTHER_1, SELF, SAME_2, EXTRA, SAME_3, SAME_1 = range(8)
SLOTS = 8
CHIPS_BACK = {OTHER_2: 2, SAME_2: 2, OTHER_1: 1, OTHER_3: 3, SAME_3: 3, SAME_1: 1}
SHARES = 4
TOGETHER = 3
KEY, VALUE = range(2)


def kernel(
    sizes,
    q_in, k_in, v_in, g_in, seg_in,
    dq_out, shares,
    seg, queries, grads, keys, values, keys_t, kinds, unkind,
    scores, pgrads, tops, sums, crosses, ds_half, p_half, dq_half,
    fresh, hold, part, part_other, chain,
    seg_sem, q_sem, g_sem, kv_sem, qg_send, kv_send, fwd_send, fwd_other_send,
    part_send, other_sem, chain_sem, share_sem, dq_send, dq_sem,
):
    head_count, inner_count, outer_count, group = sizes
    head = lax.axis_index("head")
    inner = lax.axis_index("inner")
    outer = lax.axis_index("outer")
    core = outer % CORES
    per_inner = outer_count // CORES
    chips = inner_count * per_inner
    chip = inner * per_inner + outer // CORES
    shards = chips * CORES
    place = chip * CORES + core
    tokens = q_in.shape[0]
    rows = head_count * tokens

    def at_chip(step, on_core):
        to = (chip + step + chips) % chips
        return (head, to // per_inner, (to % per_inner) * CORES + on_core)

    def at_head(step):
        to = (head + step) % head_count
        return to, (to, inner, outer)

    def wait_for(ref, sem):
        pltpu.make_async_copy(ref, ref, sem).wait()

    def send(src, dst, send_sem, recv_sem, to):
        pltpu.make_async_remote_copy(
            src_ref=src, dst_ref=dst, send_sem=send_sem, recv_sem=recv_sem,
            device_id=to, device_id_type=MESH,
        ).start()

    other = at_chip(0, 1 - core)
    next_1, next_3 = at_chip(1, core), at_chip(3, core)
    back_1, back_3 = at_chip(-1, core), at_chip(-3, core)
    extra_to = at_chip(4 * core, 1 - core)
    extra_from = at_chip(-4 * (1 - core), 1 - core)

    load_seg = pltpu.make_async_copy(seg_in, seg, seg_sem)
    load_seg.start()

    barrier = pltpu.get_barrier_semaphore()
    partners = [at_head(step)[1] for step in range(1, head_count)]
    partners += [other, next_1, next_3, back_1, back_3]
    far = at_chip(8 * core - 4, 1 - core)
    for partner in partners + [far]:
        pl.semaphore_signal(barrier, inc=1, device_id=partner, device_id_type=MESH)
    pl.semaphore_wait(barrier, len(partners) + 1)

    mine = pl.ds(pl.multiple_of(head * tokens, tokens), tokens)

    def head_columns(number):
        return pl.ds(pl.multiple_of(number * HEAD_SIZE, HEAD_SIZE), HEAD_SIZE)

    for kind, (src, dst) in enumerate(((k_in, keys), (v_in, values))):
        for step in range(1, head_count):
            to, device = at_head(step)
            send(
                src.at[:, head_columns(to)], dst.at[SELF, mine, :],
                kv_send.at[kind], kv_sem.at[SELF, kind], device,
            )
        pltpu.make_async_copy(
            src.at[:, head_columns(head)], dst.at[SELF, mine, :], kv_sem.at[SELF, kind]
        ).start()

    def send_head(number, carry):
        target = pl.ds(pl.multiple_of(number * rows + head * tokens, tokens), tokens)
        for kind, (src, dst, sem) in enumerate(
            ((q_in, queries, q_sem), (g_in, grads, g_sem))
        ):
            for step in range(1, head_count):
                to, device = at_head(step)
                send(
                    src.at[:, head_columns(to * group + number)], dst.at[target, :],
                    qg_send.at[kind], sem.at[number], device,
                )
            pltpu.make_async_copy(
                src.at[:, head_columns(head * group + number)], dst.at[target, :], sem.at[number]
            ).start()
        return carry

    lax.fori_loop(0, group, send_head, 0)

    load_seg.wait()
    lanes = seg.shape[1]
    seg_rows = rows // lanes
    session = lax.broadcasted_iota(jnp.int32, (KINDS, lanes), 0)

    def shard_of(slot):
        if slot == SELF:
            return place
        if slot == EXTRA:
            return (place - 7 + 6 * core + shards) % shards
        on_core = core if slot in (SAME_1, SAME_2, SAME_3) else 1 - core
        return ((chip - CHIPS_BACK[slot] + chips) % chips) * CORES + on_core

    for slot in range(SLOTS):
        for part_row in range(seg_rows):
            ids = seg[pl.ds(shard_of(slot) * seg_rows + part_row, 1), :]
            ones = jnp.where(session == ids, 1.0, 0.0).astype(jnp.float32).T
            span = slice(part_row * lanes, (part_row + 1) * lanes)
            kinds[slot, span, :] = ones.astype(jnp.bfloat16)
            if slot == SELF:
                unkind[span, :] = ((ones - 1.0) * FAR).astype(jnp.bfloat16)

    both = ((KEY, keys), (VALUE, values))
    onward = {SAME_1: (0, next_1), SAME_3: (1, next_3), EXTRA: (2, extra_to)}

    def pass_on(slot, kind):
        number, to = onward[slot]
        array = both[kind][1]
        send(
            array.at[SELF], array.at[slot],
            fwd_send.at[number, kind], kv_sem.at[slot, kind], to,
        )

    def arrived(slot, kind):
        wait_for(both[kind][1].at[slot], kv_sem.at[slot, kind])

    arrived(SELF, KEY)
    pass_on(SAME_1, KEY)
    arrived(SELF, VALUE)
    pass_on(SAME_3, VALUE)
    pass_on(SAME_1, VALUE)
    pass_on(SAME_3, KEY)
    pass_on(EXTRA, KEY)
    pass_on(EXTRA, VALUE)

    def hand_over(slot, slot_there, number, kind):
        array = both[kind][1]
        send(
            array.at[slot], array.at[slot_there],
            fwd_other_send.at[number, kind], kv_sem.at[slot_there, kind], other,
        )

    def relay(slot, kind, to):
        array = both[kind][1]
        send(
            array.at[slot], array.at[SAME_2], fwd_send.at[3, kind], kv_sem.at[SAME_2, kind], to
        )

    score_scale = HEAD_SIZE ** (-0.5)
    exponent = score_scale * LOG2_E
    over_last = (((1,), (1,)), ((), ()))

    def folded(block):
        return block.reshape(rows // 8, 8, block.shape[1])

    def head_span(number):
        return pl.ds(pl.multiple_of(number * rows, rows), rows)

    def turn_keys(slot):
        turned = keys[slot].astype(jnp.float32).T.astype(jnp.bfloat16)
        if isinstance(slot, int):
            keys_t[:, slot * rows : (slot + 1) * rows] = turned
        else:
            keys_t[:, head_span(slot)] = turned

    def forward(slot, heads, masked):
        wide_keys = jnp.concatenate([keys[slot], kinds[slot]], axis=1)
        here = pl.ds(slot, 1)
        for first in range(heads.start, heads.stop, TOGETHER):
            count = min(TOGETHER, heads.stop - first)
            span = slice(first * rows, (first + count) * rows)
            wide_queries = jnp.concatenate(
                [queries[span, :], jnp.concatenate([unkind[...]] * count, axis=0)], axis=1
            )
            block = lax.dot_general(
                wide_keys, wide_queries, over_last, preferred_element_type=jnp.float32
            )
            if masked:
                key_row = lax.broadcasted_iota(jnp.int32, (rows, rows), 0)
                query_column = lax.broadcasted_iota(jnp.int32, (rows, rows), 1)
                earlier = jnp.concatenate([key_row <= query_column] * count, axis=1)
                block = jnp.where(earlier, block, -FAR)
            slopes = lax.dot_general(
                values[slot], grads[span, :], over_last, preferred_element_type=jnp.float32
            )
            top = jnp.max(jnp.max(folded(block), axis=0), axis=0, keepdims=True)
            weights = jnp.exp2((block - top) * exponent)
            scores[slot, :, span] = weights
            pgrads[slot, :, span] = slopes
            tops[here, span] = top
            sums[here, span] = jnp.sum(jnp.sum(folded(weights), axis=0), axis=0, keepdims=True)
            crosses[here, span] = jnp.sum(
                jnp.sum(folded(weights * slopes), axis=0), axis=0, keepdims=True
            )

    def own_block(heads):
        for number in heads:
            wait_for(queries.at[head_span(number), :], q_sem.at[number])
            wait_for(grads.at[head_span(number), :], g_sem.at[number])
            forward(SELF, range(number, number + 1), True)

    turn_keys(SELF)
    own_block(range(0, group // 2))
    arrived(SAME_1, KEY)
    relay(SAME_1, KEY, next_1)
    hand_over(SAME_1, OTHER_1, 0, KEY)
    arrived(SAME_3, VALUE)
    relay(SAME_3, VALUE, back_1)
    hand_over(SAME_3, OTHER_3, 1, VALUE)
    own_block(range(group // 2, group - 1))
    arrived(SAME_1, VALUE)
    hand_over(SAME_1, OTHER_1, 0, VALUE)
    arrived(SAME_3, KEY)
    hand_over(SAME_3, OTHER_3, 1, KEY)
    own_block(range(group - 1, group))

    def only(condition):
        return (lambda work: work()) if condition else (lambda work: None)

    def forward_next(slot):
        @only(slot == EXTRA)
        def _():
            for kind in (KEY, VALUE):
                arrived(SAME_2, kind)
                hand_over(SAME_2, OTHER_2, 2, kind)

        for late in (EXTRA, OTHER_1, OTHER_3, OTHER_2):

            @only(slot == late)
            def _():
                for kind in (KEY, VALUE):
                    arrived(late, kind)

        turn_keys(slot)
        forward(slot, range(group), False)

    for slot in (SAME_1, SAME_3, EXTRA, SAME_2, OTHER_1, OTHER_3, OTHER_2):
        forward_next(slot)

    top = tops[...]
    factor = jnp.exp2((top - jnp.max(top, axis=0, keepdims=True)) * exponent)
    total = jnp.sum(factor * sums[...], axis=0, keepdims=True)
    cross = jnp.sum(factor * crosses[...], axis=0, keepdims=True)
    tops[...] = factor / total
    sums[0:1, :] = cross / total

    def to_owners(slot, kind, number, step, on_core, first):
        for hop in range(first, head_count):
            to, _ = at_head(hop)
            here = pl.ds(pl.multiple_of(to * tokens, tokens), tokens)
            send(
                part.at[slot, kind, here, :], shares.at[number, head, kind],
                part_send.at[slot], share_sem, (to, *at_chip(step, on_core)[1:]),
            )

    def backward(slot):
        for first in range(0, group, TOGETHER):
            span = slice(first * rows, min(first + TOGETHER, group) * rows)
            probs = scores[slot, :, span] * tops[pl.ds(slot, 1), span]
            p_half[:, span] = probs.astype(jnp.bfloat16)
            ds_half[slot, :, span] = (probs * (pgrads[slot, :, span] - sums[0:1, span])).astype(
                jnp.bfloat16
            )
        fresh[KEY] = jnp.dot(ds_half[slot], queries[...], preferred_element_type=jnp.float32)
        fresh[VALUE] = jnp.dot(p_half[...], grads[...], preferred_element_type=jnp.float32)
        part[slot] = fresh[...].astype(jnp.bfloat16)

        for here, number in ((OTHER_2, 2), (OTHER_3, 1), (OTHER_1, 0)):

            @only(slot == here)
            def _():
                send(
                    part.at[here], part_other.at[number], part_send.at[here],
                    other_sem.at[number], other,
                )

        def add_other(here, kind, number):
            return fresh[kind] + part_other[number, kind].astype(jnp.float32)

        @only(slot == SAME_2)
        def _():
            wait_for(part_other.at[2], other_sem.at[2])
            for kind, to in ((KEY, back_1), (VALUE, next_1)):
                part[SAME_2, kind] = add_other(SAME_2, kind, 2).astype(jnp.bfloat16)
                send(
                    part.at[SAME_2, kind], chain.at[kind], part_send.at[SAME_2],
                    chain_sem.at[kind], to,
                )

        @only(slot == EXTRA)
        def _():
            for kind in (KEY, VALUE):
                to_owners(EXTRA, kind, 2, -4 * (1 - core), 1 - core, 0)

        for here, number, kind, step in ((SAME_3, 1, KEY, -3), (SAME_1, 0, VALUE, -1)):

            @only(slot == here)
            def _():
                wait_for(part_other.at[number], other_sem.at[number])
                part[here, kind] = add_other(here, kind, number).astype(jnp.bfloat16)
                to_owners(here, kind, number, step, core, 0)
                hold[1 - kind] = add_other(here, 1 - kind, number)

        @only(slot == SELF)
        def _():
            for kind in (KEY, VALUE):
                to_owners(SELF, kind, 3, 0, core, 1)
                pltpu.make_async_copy(
                    part.at[SELF, kind, mine, :], shares.at[3, head, kind], share_sem
                ).start()


    for slot in (OTHER_2, OTHER_3, OTHER_1, SAME_2, SELF, EXTRA, SAME_3, SAME_1):
        backward(slot)

    def send_back(number, carry):
        blocks = ds_half[:, :, head_span(number)].reshape(SLOTS * rows, rows)
        dq = jnp.dot(keys_t[...], blocks, preferred_element_type=jnp.float32).T * score_scale
        dq_half[head_span(number), :] = dq.astype(jnp.bfloat16)
        columns = head_columns(head * group + number)
        for step in range(1, head_count):
            to, device = at_head(step)
            here = pl.ds(pl.multiple_of(number * rows + to * tokens, tokens), tokens)
            send(dq_half.at[here, :], dq_out.at[:, columns], dq_send, dq_sem, device)
        here = pl.ds(pl.multiple_of(number * rows + head * tokens, tokens), tokens)
        pltpu.make_async_copy(dq_half.at[here, :], dq_out.at[:, columns], dq_sem).start()
        return carry

    def send_some(turn, carry):
        for one in range(3):
            send_back(turn * 3 + one, carry)
        return carry

    lax.fori_loop(0, group // 3, send_some, 0)

    for slot, kind, number, step in ((SAME_3, VALUE, 1, -3), (SAME_1, KEY, 0, -1)):
        wait_for(chain.at[kind], chain_sem.at[kind])
        part[slot, kind] = (hold[kind] + chain[kind].astype(jnp.float32)).astype(jnp.bfloat16)
        to_owners(slot, kind, number, step, core, 0)

    peers = head_count - 1
    for kind, (src, kv) in enumerate(((q_in, k_in), (g_in, v_in))):
        wait_for(src.at[:, : peers * group * HEAD_SIZE], qg_send.at[kind])
        wait_for(kv.at[:, : peers * HEAD_SIZE], kv_send.at[kind])
        array = (keys, values)[kind]
        for number in range(4):
            wait_for(array.at[SELF], fwd_send.at[number, kind])
        for number in range(3):
            wait_for(array.at[SELF], fwd_other_send.at[number, kind])
    for slot in range(SLOTS):
        if slot != SELF:
            wait_for(part.at[slot], part_send.at[slot])
    wait_for(part.at[SELF, :, : peers * tokens, :], part_send.at[SELF])
    wait_for(dq_out.at[:, : peers * group * HEAD_SIZE], dq_send)
    wait_for(dq_out, dq_sem)
    wait_for(shares, share_sem)


def finish(dq_in, shares, dq_out, dk_out, dv_out):
    dq_out[...] = dq_in[...]
    heads = shares.shape[1]
    for kind, out in enumerate((dk_out, dv_out)):
        for head in range(heads):
            total = shares[0, head, kind].astype(jnp.float32)
            for number in range(1, SHARES):
                total = total + shares[number, head, kind].astype(jnp.float32)
            if kind == KEY:
                total = total * HEAD_SIZE ** (-0.5)
            out[:, head * HEAD_SIZE : (head + 1) * HEAD_SIZE] = total.astype(jnp.bfloat16)


def body(query_heads, key_heads, value_matrix, out_grad, segment_ids):
    head_count = lax.axis_size("head")
    sizes = (head_count, lax.axis_size("inner"), lax.axis_size("outer"), query_heads.shape[1] // key_heads.shape[1])
    group = sizes[3]
    tokens = query_heads.shape[0]
    rows = head_count * tokens
    half, full = jnp.bfloat16, jnp.float32
    ids = segment_ids.reshape(-1, 128)
    dma = pltpu.SemaphoreType.DMA
    anywhere = pl.BlockSpec(memory_space=pl.ANY)
    dq, shares = pl.pallas_call(
        functools.partial(kernel, sizes),
        out_shape=(
            jax.ShapeDtypeStruct(query_heads.shape, half),
            jax.ShapeDtypeStruct((SHARES, head_count, 2, tokens, HEAD_SIZE), half),
        ),
        in_specs=[anywhere] * 5,
        out_specs=[anywhere] * 2,
        scratch_shapes=[
            pltpu.VMEM(ids.shape, jnp.int32),
            pltpu.VMEM((group * rows, HEAD_SIZE), half),
            pltpu.VMEM((group * rows, HEAD_SIZE), half),
            pltpu.VMEM((SLOTS, rows, HEAD_SIZE), half),
            pltpu.VMEM((SLOTS, rows, HEAD_SIZE), half),
            pltpu.VMEM((HEAD_SIZE, SLOTS * rows), half),
            pltpu.VMEM((SLOTS, rows, KINDS), half),
            pltpu.VMEM((rows, KINDS), half),
            pltpu.VMEM((SLOTS, rows, group * rows), full),
            pltpu.VMEM((SLOTS, rows, group * rows), full),
            pltpu.VMEM((SLOTS, group * rows), full),
            pltpu.VMEM((SLOTS, group * rows), full),
            pltpu.VMEM((SLOTS, group * rows), full),
            pltpu.VMEM((SLOTS, rows, group * rows), half),
            pltpu.VMEM((rows, group * rows), half),
            pltpu.VMEM((group * rows, HEAD_SIZE), half),
            pltpu.VMEM((2, rows, HEAD_SIZE), full),
            pltpu.VMEM((2, rows, HEAD_SIZE), full),
            pltpu.VMEM((SLOTS, 2, rows, HEAD_SIZE), half),
            pltpu.VMEM((3, 2, rows, HEAD_SIZE), half),
            pltpu.VMEM((2, rows, HEAD_SIZE), half),
            dma,
            dma((group,)),
            dma((group,)),
            dma((SLOTS, 2)),
            dma((2,)),
            dma((2,)),
            dma((4, 2)),
            dma((3, 2)),
            dma((SLOTS,)),
            dma((3,)),
            dma((2,)),
            dma,
            dma,
            dma,
        ],
        compiler_params=pltpu.CompilerParams(
            collective_id=0, has_side_effects=True, vmem_limit_bytes=56 * 2**20
        ),
    )(query_heads, key_heads, value_matrix, out_grad, ids)
    return pl.pallas_call(
        finish,
        out_shape=(
            jax.ShapeDtypeStruct(query_heads.shape, half),
            jax.ShapeDtypeStruct(key_heads.shape, half),
            jax.ShapeDtypeStruct(value_matrix.shape, half),
        ),
    )(dq, shares)


def solution(mesh):
    split = P(("inner", "outer", "head"), None)
    return jax.shard_map(
        body,
        mesh=mesh,
        in_specs=(split, split, split, split, P()),
        out_specs=(split, split, split),
        check_vma=False,
    )
```
